32 devices in a mesh: grp: 2 (over x), lat: 16 (over z, y, core).
Axes of the slice: x: 2, y: 2, z: 4, core: 2. Of those that a mesh axis runs over, the one named last changes fastest.
Arguments:
- grid_values: bfloat16 [32, 64, 304], P('grp', None, 'lat'), parts along dimension 0, may hold values from -6 to 6
- quad_weights: float32 [128], replicated, may hold values from 0.5 to 4
- owner_map: int32 [512], replicated, may hold values from 0 to 15, as said below
- legendre: bfloat16 [512, 512, 128], P('lat'), may hold values from -0.5 to 0.5
- diffusion: float32 [4], replicated, may hold values from 1 to 16
Outputs:
- grid_result: bfloat16 [32, 64, 304], P('grp', None, 'lat'), parts along dimension 0
The draws below stay inside these ranges and needn't reach their ends.
There are 2 independent parts, one for each index of `grp`. The reference program is written for one: setup_inputs(seed, part) draws one part's arguments, and reference() takes and returns one part's arrays. A program takes and returns all parts, laid end to end along the dimension named above; an argument that names none is the same for every part. Nothing has to cross between parts.
Inputs may be any that keep to these rules, and one draw needn't show every extreme that they name: `owner_map`: every index of lat owns exactly 32 wavenumbers; m and 511 - m have the same owner.
All inputs are finite; a program needn't handle non-finite values.
Results may differ from the reference program's by a relative error of at most 0.007.
Values may be sent and summed in bfloat16 or wider, within the bound.
No kernel may reach another device: no remote copies, remote signals or barrier semaphores. Data moves between devices by JAX's collectives and lax.ppermute only.
A program may use at most 128 MiB of HBM per device.

```python
import math
import jax
import jax.numpy as jnp
from jax import lax

M = 512
FIELDS = 4
LEVELS = 4
CHAN = 16
NLAT = 128
HALF = 64
ROWMAX = 304
N_LAT = 16


def draw_owner_map(key, part):
    key = jax.random.fold_in(key, 23)
    half_count = M // 2
    shuffled = jax.random.permutation(key, half_count)
    per_owner = M // N_LAT // 2
    owner_pair = jnp.zeros((half_count,), jnp.int32).at[shuffled].set(jnp.arange(half_count, dtype=jnp.int32) // per_owner)
    return jnp.concatenate([owner_pair, owner_pair[::-1]]).astype(jnp.int32)


def levels(rng, shape, pieces, least, top_value):
    level, own = 1.0, jax.random.fold_in(rng, 6)
    for dim, shards_of in pieces:
        heights = jnp.exp(jax.random.uniform(jax.random.fold_in(own, dim), (shards_of,), jnp.float32, least / len(pieces), top_value / len(pieces)))
        level = level * jnp.repeat(heights, shape[dim] // shards_of).reshape([-1 if axis == dim else 1 for axis in range(len(shape))])
    return level


def gaussian(own_key, dims, scale, reach, cuts=(), kind=jnp.bfloat16):
    entries = jax.random.normal(own_key, dims, jnp.float32) * scale
    if len(cuts) > 0:
        entries = levels(own_key, dims, cuts, -0.22, 0.18) * entries
    return jnp.clip(entries, min=-reach, max=reach).astype(kind)


def setup_inputs(seed: int = 0, part: int = 0) -> dict:
    key_of = jax.random.split(jax.random.key(seed), 6)
    own_keys = jax.random.split(jax.random.fold_in(key_of[5], part), 6)
    grid_values = gaussian(own_keys[0], (CHAN, HALF, ROWMAX), 1.0, 6.0, ((2, 16),))
    quad_weights = jnp.clip(jnp.exp(jax.random.uniform(key_of[1], (NLAT,), jnp.float32, math.log(0.5), math.log(4.0))), 0.5, 4.0)
    owner_map = draw_owner_map(jax.random.fold_in(key_of[5], 71), part)
    legendre = gaussian(key_of[3], (M, M, NLAT), (M // 4) ** -0.5, 0.5, ((0, 16),))
    diffusion = jnp.clip(jnp.exp(jax.random.uniform(key_of[4], (FIELDS,), jnp.float32, math.log(1.0), math.log(16.0))), 1.0, 16.0)
    return dict(grid_values=grid_values, quad_weights=quad_weights, owner_map=owner_map, legendre=legendre, diffusion=diffusion)


TWO_PI = 2.0 * math.pi


def pair_rows(lat_total):
    half = lat_total // 2
    quarter = lat_total // 4
    pair_ids = jnp.arange(half, dtype=jnp.int32)
    north = pair_ids < quarter
    shifted = pair_ids - quarter
    first = jnp.where(north, pair_ids, half + shifted).astype(jnp.int32)
    second = jnp.where(north, half - 1 - pair_ids, lat_total - 1 - shifted).astype(jnp.int32)
    return first, second


def row_length(lat_ids, lat_total):
    return (20 + 4 * jnp.minimum(lat_ids, lat_total - 1 - lat_ids)).astype(jnp.int32)


def trig_table(length, offset, col_start, col_count, wave_ids):
    col_ids = col_start + jnp.arange(col_count, dtype=jnp.int32)
    local = col_ids - offset
    phases = (local[:, None] * wave_ids[None, :]) % length
    angles = (phases.astype(jnp.float32) / length.astype(jnp.float32)) * TWO_PI
    usable = (local[:, None] >= 0) & (local[:, None] < length) & (2 * wave_ids[None, :] < length)
    cos_part = jnp.where(usable, jnp.cos(angles), 0.0).astype(jnp.bfloat16)
    sin_part = jnp.where(usable, jnp.sin(angles), 0.0).astype(jnp.bfloat16)
    return jnp.concatenate([cos_part, sin_part], axis=1)


def reference(grid_values, quad_weights, owner_map, legendre, diffusion):
    channels = grid_values.shape[0]
    row_width = grid_values.shape[2]
    wave_ids = jnp.arange(M, dtype=jnp.int32)
    slot_order = jnp.argsort(owner_map, stable=True).astype(jnp.int32)
    first, second = pair_rows(NLAT)
    first_len = row_length(first, NLAT)
    second_len = row_length(second, NLAT)
    rows_each = HALF // N_LAT

    def scaled(totals, weight, length):
        row_scale = weight / length.astype(jnp.float32)
        return jnp.concatenate([totals[:, :M] * row_scale, totals[:, M:] * (-row_scale)], axis=1).astype(jnp.bfloat16)

    def forward(packed):
        row_data, len_a, len_b, weight_a, weight_b = packed
        table_a = trig_table(len_a, 0, 0, row_width, wave_ids)
        table_b = trig_table(len_b, len_a, 0, row_width, wave_ids)
        totals_a = jnp.dot(row_data, table_a, preferred_element_type=jnp.float32)
        totals_b = jnp.dot(row_data, table_b, preferred_element_type=jnp.float32)
        return jnp.stack([scaled(totals_a, weight_a, len_a), scaled(totals_b, weight_b, len_b)])

    per_pair = lax.map(forward, (jnp.swapaxes(grid_values, 0, 1), first_len, second_len, quad_weights[first], quad_weights[second]))
    fourier = per_pair.reshape(N_LAT, rows_each, 2, channels, 2 * M)
    fourier = jnp.transpose(fourier, (0, 2, 1, 3, 4)).reshape(NLAT, channels, 2, M)
    picked = jnp.moveaxis(fourier[:, :, :, slot_order], 3, 0)
    rates = jnp.repeat(diffusion, LEVELS)
    degree = jnp.arange(M, dtype=jnp.int32)
    ladder = (degree * (degree + 1)).astype(jnp.float32)
    factor = 1.0 / (1.0 + rates[:, None] * (ladder[None, :] / float(M * (M - 1))))

    def per_slot(packed):
        table_slot, coeffs, wave_id = packed
        spectral = jnp.dot(table_slot, coeffs.reshape(NLAT, 2 * channels), preferred_element_type=jnp.float32)
        spectral = spectral.reshape(M, channels, 2)
        damping = jnp.where(degree[None, :] >= wave_id, factor, 0.0)
        filtered = (spectral * jnp.swapaxes(damping, 0, 1)[:, :, None]).astype(jnp.bfloat16)
        back = jnp.dot(jnp.swapaxes(table_slot, 0, 1), filtered.reshape(M, 2 * channels), preferred_element_type=jnp.float32)
        return back.astype(jnp.bfloat16).reshape(NLAT, channels, 2)

    back_rows = lax.map(per_slot, (legendre, picked, slot_order))
    by_wave = jnp.zeros_like(back_rows).at[slot_order].set(back_rows)
    by_pos = jnp.moveaxis(by_wave, 1, 0)
    by_pair = by_pos.reshape(N_LAT, 2, rows_each, M, channels, 2)
    by_pair = jnp.transpose(by_pair, (0, 2, 1, 3, 4, 5)).reshape(HALF, 2, M, channels, 2)
    double = jnp.where(wave_ids == 0, 1.0, 2.0).astype(jnp.bfloat16)

    def stack_parts(coeffs):
        return jnp.concatenate([coeffs[:, :, 0] * double[:, None], -(coeffs[:, :, 1] * double[:, None])], axis=0)

    def inverse(packed):
        coeffs_a, coeffs_b, len_a, len_b = packed
        table_a = trig_table(len_a, 0, 0, row_width, wave_ids)
        table_b = trig_table(len_b, len_a, 0, row_width, wave_ids)
        total = jnp.dot(table_a, stack_parts(coeffs_a), preferred_element_type=jnp.float32)
        total = total + jnp.dot(table_b, stack_parts(coeffs_b), preferred_element_type=jnp.float32)
        return total.astype(jnp.bfloat16)

    rows_out = lax.map(inverse, (by_pair[:, 0], by_pair[:, 1], first_len, second_len))
    return jnp.transpose(rows_out, (2, 0, 1))
```

```python
import functools
import math

import jax
import jax.numpy as jnp
from jax import lax
from jax.experimental import pallas as pl
from jax.experimental.pallas import tpu as pltpu
from jax.sharding import PartitionSpec as P

LEVELS = 4


TWO_PI = 2.0 * math.pi


def pair_rows(lat_total):
    half = lat_total // 2
    quarter = lat_total // 4
    pair_ids = jnp.arange(half, dtype=jnp.int32)
    north = pair_ids < quarter
    shifted = pair_ids - quarter
    first = jnp.where(north, pair_ids, half + shifted)
    second = jnp.where(north, half - 1 - pair_ids, lat_total - 1 - shifted)
    return (first, second)


def row_length(lat_ids, lat_total):
    return 20 + 4 * jnp.minimum(lat_ids, lat_total - 1 - lat_ids)


def trig_table(length, offset, col_count, wave_ids):
    col_ids = jnp.arange(col_count, dtype=jnp.int32)
    local = col_ids - offset
    phases = local[:, None] * wave_ids[None, :] % length
    angles = phases.astype(jnp.float32) / length.astype(jnp.float32) * TWO_PI
    usable = (local[:, None] >= 0) & (local[:, None] < length) & (2 * wave_ids[None, :] < length)
    cos_part = jnp.where(usable, jnp.cos(angles), 0.0).astype(jnp.bfloat16)
    sin_part = jnp.where(usable, jnp.sin(angles), 0.0).astype(jnp.bfloat16)
    return jnp.concatenate([cos_part, sin_part], axis=1)


def any_rows_body(grid_values, quad_weights, owner_map, legendre, diffusion):
    channels, half_total, col_dev = grid_values.shape
    groups = lax.axis_size("lat")
    device = lax.axis_index("lat")
    half_dev = half_total // groups
    lat_total = 2 * half_total
    row_width = col_dev * groups
    owned_slots = legendre.shape[0]
    wave_count = legendre.shape[1]
    wave_ids = jnp.arange(wave_count, dtype=jnp.int32)
    slot_order = jnp.argsort(owner_map, stable=True)
    inverse_order = jnp.argsort(slot_order)
    my_waves = lax.dynamic_slice_in_dim(slot_order, device * owned_slots, owned_slots)
    contract = (((0,), (1,)), ((), ()))
    first, second = pair_rows(lat_total)
    my_first = lax.dynamic_slice_in_dim(first, device * half_dev, half_dev)
    my_second = lax.dynamic_slice_in_dim(second, device * half_dev, half_dev)
    first_len = row_length(my_first, lat_total)
    second_len = row_length(my_second, lat_total)
    first_weight = jnp.take(quad_weights, my_first)
    second_weight = jnp.take(quad_weights, my_second)

    def pair_tables(packed):
        len_a, len_b = packed
        return jnp.concatenate(
            [
                trig_table(len_a, 0, row_width, wave_ids),
                trig_table(len_b, len_a, row_width, wave_ids),
            ],
            axis=1,
        )

    all_tables = lax.map(pair_tables, (first_len, second_len))

    def forward_pair(row_data, tables):
        totals = lax.dot_general(tables, row_data, contract, preferred_element_type=jnp.float32)
        return (totals[: 2 * wave_count], totals[2 * wave_count :])

    def inverse_pair(coeffs_a, coeffs_b, tables):
        joined = jnp.concatenate([coeffs_a, coeffs_b], axis=0)
        return lax.dot_general(joined, tables, contract, preferred_element_type=jnp.float32).astype(
            jnp.bfloat16
        )

    def scaled(totals, weight, length):
        row_scale = weight / length.astype(jnp.float32)
        return jnp.concatenate(
            [totals[:wave_count] * row_scale, totals[wave_count:] * -row_scale], axis=0
        ).astype(jnp.bfloat16)

    def forward_one_pair(packed):
        row_data, tables, len_a, len_b, weight_a, weight_b = packed
        totals_a, totals_b = forward_pair(row_data, tables)
        return jnp.stack([scaled(totals_a, weight_a, len_a), scaled(totals_b, weight_b, len_b)])

    per_pair = lax.map(
        forward_one_pair,
        (
            jnp.moveaxis(
                lax.all_to_all(grid_values, "lat", split_axis=1, concat_axis=2, tiled=True), 1, 0
            ),
            all_tables,
            first_len,
            second_len,
            first_weight,
            second_weight,
        ),
    )
    per_lat = per_pair.transpose(1, 0, 2, 3).reshape(2 * half_dev, 2, wave_count, -1)
    fourier = per_lat.transpose(2, 1, 3, 0)
    picked = fourier[slot_order]
    rates = jnp.repeat(diffusion, LEVELS)
    degree = jnp.arange(wave_count, dtype=jnp.int32)
    ladder = (degree * (degree + 1)).astype(jnp.float32)
    factor = 1.0 / (1.0 + rates[:, None] * (ladder[None, :] / float(wave_count * (wave_count - 1))))
    damping = jnp.where((degree[None, :] >= my_waves[:, None])[:, None, :], factor[None, :, :], 0.0)
    spectral = jnp.einsum(
        "snl,spcl->spcn",
        legendre,
        lax.all_to_all(picked, "lat", split_axis=0, concat_axis=3, tiled=True),
        preferred_element_type=jnp.float32,
    )
    filtered = (spectral * damping[:, None, :, :]).astype(jnp.bfloat16)
    back = jnp.einsum("snl,spcn->spcl", legendre, filtered, preferred_element_type=jnp.float32)
    returned = back.astype(jnp.bfloat16)
    double = jnp.where(wave_ids == 0, 1.0, 2.0).astype(jnp.bfloat16)
    by_wave = lax.all_to_all(returned, "lat", split_axis=3, concat_axis=0, tiled=True)[
        inverse_order
    ]
    real_part = by_wave[:, 0] * double[:, None, None]
    imag_part = -(by_wave[:, 1] * double[:, None, None])
    stacked = jnp.concatenate([real_part, imag_part], axis=0)

    def backward_one_pair(packed):
        coeffs_a, coeffs_b, tables, len_a, len_b = packed
        return inverse_pair(coeffs_a, coeffs_b, tables)

    per_pair = lax.map(
        backward_one_pair,
        (
            jnp.moveaxis(stacked[:, :, :half_dev], 2, 0),
            jnp.moveaxis(stacked[:, :, half_dev:], 2, 0),
            all_tables,
            first_len,
            second_len,
        ),
    )
    rows_out = jnp.moveaxis(per_pair, 0, 1)
    return lax.all_to_all(rows_out, "lat", split_axis=2, concat_axis=1, tiled=True)


SIN_POLY = (3.141592640130707, -5.1677100835078775, 2.550077523214437, -0.5982912856197345, 0.07765766030450941)
COS_POLY = (0.9999999532476085, -4.934792830619644, 4.058411352862619, -1.3318765680811142, 0.2196896110983216)
LANES = 128
SUB = 8
F32 = jnp.float32
BF16 = jnp.bfloat16


def horner(poly, u):
    total = poly[-1]
    for term in poly[-2::-1]:
        total = total * u + term
    return total


def iota(shape, axis):
    return lax.broadcasted_iota(jnp.int32, shape, axis)


def swap_blocks(v):
    sub = iota(v.shape, 1)
    lane = iota(v.shape, 2)
    for bit in range(3):
        step = 1 << bit
        row_bit = (sub >> bit) & 1
        lane_bit = (lane >> (3 + bit)) & 1
        up = pltpu.roll(pltpu.roll(v, SUB - step, 1), SUB * step, 2)
        down = pltpu.roll(pltpu.roll(v, step, 1), LANES - SUB * step, 2)
        v = jnp.where(row_bit == lane_bit, v, jnp.where(row_bit == 0, up, down))
    return v


def pack_kernel(x_ref, o_ref):
    cols, channels, rows = x_ref.shape
    half = channels // 2
    x = x_ref[...].astype(F32)
    v = swap_blocks(jnp.concatenate([x[:, :half], x[:, half:]], axis=2))
    y = v.reshape(cols * SUB, LANES).astype(BF16)
    for chip in range(o_ref.shape[0]):
        o_ref[chip] = y


def unpack_kernel(x_ref, o_ref):
    cols, channels, rows = o_ref.shape
    half = channels // 2
    total = x_ref[0].astype(F32)
    for chip in range(1, x_ref.shape[0]):
        total = total + x_ref[chip].astype(F32)
    v = swap_blocks(total.reshape(cols, SUB, LANES))
    o_ref[:, :half] = v[:, :, :rows].astype(BF16)
    o_ref[:, half:] = v[:, :, rows:].astype(BF16)


def row_lengths(r, half_total):
    quarter = half_total // 2
    lat_total = 2 * half_total
    north = r < quarter
    first = jnp.where(north, r, half_total + r - quarter)
    second = jnp.where(north, half_total - 1 - r, lat_total - 1 - (r - quarter))
    return row_length(first, lat_total), row_length(second, lat_total), first, second


def table_kernel(
    half_total, cols, waves, device_ref, owner_ref, weight_ref, rate_ref, tt_ref, tr_ref, wave_ref, scale_ref, factor_ref, jf_ref
):
    points = tt_ref.shape[1]
    slots = wave_ref.shape[0]
    pairs = points // (2 * cols)
    device = device_ref[0]
    core = device % 2
    low = waves // 2
    owned = jnp.where(owner_ref[:, :low] == device, 1.0, 0.0)
    owned = jnp.broadcast_to(owned, (LANES, low)).T
    below = jnp.where(iota((low, low), 1) <= iota((low, low), 0), 1.0, 0.0).astype(BF16)
    count = jnp.dot(below, owned.astype(BF16), preferred_element_type=F32)
    wave_id = iota((low, LANES), 0).astype(F32)
    lane_slot = (iota((low, LANES), 1) % slots).astype(F32)
    hit = (owned > 0.5) & (count - 1.0 == lane_slot)
    wave = jnp.sum(jnp.where(hit, wave_id, 0.0), axis=0, keepdims=True)
    wave_ref[...] = jnp.broadcast_to(wave, (LANES, LANES)).T[:slots]
    lat_total = 2 * half_total
    weight = jnp.broadcast_to(weight_ref[...], (LANES, lat_total)).T
    line = iota((lat_total, LANES), 0)
    lat_len = row_length(line, lat_total).astype(F32)
    scale = weight / lat_len
    lane_row = iota((SUB, LANES), 1) % SUB
    keep = lane_row == iota((SUB, LANES), 0)
    quarter = half_total // 2
    flip_row = SUB - 1 - iota((SUB, SUB), 0)
    for t in range(half_total // SUB):
        r = SUB * t
        if r < quarter:
            first, second = r, half_total - 1 - r
        else:
            first, second = half_total + r - quarter, lat_total - 1 - (r - quarter)
        top = scale[first : first + SUB]
        under = scale[second - SUB + 1 : second + 1]
        under = jnp.concatenate([under[SUB - 1 - i : SUB - i] for i in range(SUB)], axis=0)
        scale_ref[2 * t] = jnp.where(keep, top, 0.0)
        scale_ref[2 * t + 1] = jnp.where(keep, under, 0.0)
    degree = iota((waves, LANES), 0)
    ladder = (degree * (degree + 1)).astype(F32) / float(waves * (waves - 1))
    factor_ref[...] = 1.0 / (1.0 + rate_ref[...] * ladder)
    place = iota((points, LANES), 0)
    other = jnp.where(place >= pairs * cols, 1, 0)
    rest = place - other * (pairs * cols)
    chip = jnp.floor((rest.astype(F32) + 0.5) * (1.0 / cols)).astype(jnp.int32)
    column = (2 * chip + jnp.where(other == 1, 1 - core, core)) * cols + rest - chip * cols
    jf_ref[...] = column.astype(F32)

    def block(t, carry):
        r = SUB * t + iota((1, LANES), 1) // slots
        len_a, len_b, _, _ = row_lengths(r, half_total)
        len_a = len_a.astype(F32)
        len_b = len_b.astype(F32)
        inv_a = 1.0 / len_a
        inv_b = 1.0 / len_b
        end_a = jnp.where(2.0 * wave < len_a, len_a, 0.0)
        end_b = jnp.where(2.0 * wave < len_b, len_a + len_b, 0.0)
        for chunk in range(points // 16):
            span = slice(16 * chunk, 16 * chunk + 16)
            jf = jf_ref[span]
            in_a = jf < len_a
            length = jnp.where(in_a, len_a, len_b)
            inverse = jnp.where(in_a, inv_a, inv_b)
            phase = jnp.where(in_a, jf, jf - len_a) * wave
            turns = jnp.floor(phase * inverse + 0.5)
            part = (phase - turns * length) * inverse
            square = part * part
            half_sin = part * horner(SIN_POLY, square)
            half_cos = horner(COS_POLY, square)
            cos_part = 1.0 - 2.0 * (half_sin * half_sin)
            sin_part = 2.0 * (half_sin * half_cos)
            use_a = jf < end_a
            use_b = (jf < end_b) & jnp.logical_not(in_a)
            tt_ref[t, span, 0:LANES] = jnp.where(use_a, cos_part, 0.0).astype(BF16)
            tt_ref[t, span, LANES : 2 * LANES] = jnp.where(use_a, sin_part, 0.0).astype(BF16)
            tt_ref[t, span, 2 * LANES : 3 * LANES] = jnp.where(use_b, cos_part, 0.0).astype(BF16)
            tt_ref[t, span, 3 * LANES : 4 * LANES] = jnp.where(use_b, sin_part, 0.0).astype(BF16)
        for quarter_id in range(4):
            lanes = slice(quarter_id * LANES, (quarter_id + 1) * LANES)
            tr_ref[t, lanes, :] = tt_ref[t, :, lanes].T
        return carry

    lax.fori_loop(0, half_total // SUB, block, 0)


def main_kernel(
    own_ref, other_ref, tt_ref, tr_ref, wave_ref, scale_ref, factor_ref, leg_ref, o_ref, z_ref, at_ref, bt_ref
):
    blocks, points, _ = tt_ref.shape
    slots, waves, lat_total = leg_ref.shape
    pairs, lines, _ = own_ref.shape
    channels = LANES // SUB
    half = pairs * lines
    for chip in range(pairs):
        z_ref[chip * lines : (chip + 1) * lines] = own_ref[chip].astype(F32)
        z_ref[half + chip * lines : half + (chip + 1) * lines] = other_ref[chip].astype(F32)
    row2 = iota((2 * LANES, LANES), 0)
    col2 = iota((2 * LANES, LANES), 1)
    gather = jnp.where(row2 // SUB == col2, jnp.where(row2 < LANES, 1.0, -1.0), 0.0).astype(BF16)
    row3 = iota((LANES, 2 * LANES), 0)
    col3 = iota((LANES, 2 * LANES), 1)
    spread = jnp.where(col3 // SUB == row3, jnp.where(col3 < LANES, 1.0, -1.0), 0.0).astype(BF16)
    slab = SUB * slots // 2

    def forward(t, carry):
        z = z_ref[pl.ds(t, points, stride=SUB), :].astype(BF16)
        d = jnp.dot(tr_ref[t], z, preferred_element_type=F32)
        for h in range(2):
            parts = []
            for p in range(2):
                base = (2 * h + p) * LANES
                rows = [
                    d[base + i * slots : base + (i + 1) * slots] * scale_ref[2 * t + h, i : i + 1, :]
                    for i in range(SUB)
                ]
                parts.append(jnp.concatenate(rows, axis=0).astype(BF16))
            a = jnp.dot(jnp.concatenate(parts, axis=1), gather, preferred_element_type=F32)
            for i in range(2):
                at_ref[pl.ds(pl.multiple_of((2 * t + i) * LANES + h * slab, SUB), slab), :] = a[i * slab : (i + 1) * slab]
        return carry

    lax.fori_loop(0, blocks, forward, 0)
    degree = iota((waves, LANES), 0).astype(F32)

    def slot(s, carry):
        f = at_ref[pl.ds(s, lat_total, stride=slots), :].astype(BF16)
        table = leg_ref[s]
        spectral = jnp.dot(table, f, preferred_element_type=F32)
        wave = wave_ref[pl.ds(s, 1), :]
        kept = jnp.where(degree >= wave, spectral * factor_ref[...], 0.0).astype(BF16)
        back = lax.dot_general(table, kept, (((0,), (0,)), ((), ())), preferred_element_type=F32)
        back = back.astype(BF16).astype(F32) * jnp.where(wave == 0.0, 1.0, 2.0)
        bt_ref[pl.ds(s, lat_total, stride=slots), :] = back
        return carry

    lax.fori_loop(0, slots, slot, 0)
    keep = (iota((LANES, 2 * LANES), 1) % SUB) == iota((LANES, 2 * LANES), 0) // slots

    def inverse(t, carry):
        rhs = []
        for h in range(2):
            b = jnp.concatenate(
                [bt_ref[pl.ds(pl.multiple_of((2 * t + i) * LANES + h * slab, SUB), slab), :] for i in range(2)], axis=0
            ).astype(BF16)
            wide = jnp.dot(b, spread, preferred_element_type=F32)
            wide = jnp.where(keep, wide, 0.0).astype(BF16)
            rhs.append(wide[:, :LANES])
            rhs.append(wide[:, LANES:])
        out = jnp.dot(tt_ref[t], jnp.concatenate(rhs, axis=0), preferred_element_type=F32)
        z_ref[pl.ds(t, points, stride=SUB), :] = out
        return carry

    lax.fori_loop(0, blocks, inverse, 0)
    for chip in range(pairs):
        o_ref[0, chip] = z_ref[chip * lines : (chip + 1) * lines].astype(BF16)
        o_ref[1, chip] = z_ref[half + chip * lines : half + (chip + 1) * lines].astype(BF16)


VMEM = pltpu.MemorySpace.VMEM if hasattr(pltpu, "MemorySpace") else pltpu.VMEM


def kernel_call(body, out_shape, in_specs, scratch=(), flops=0, moved=0):
    return pl.pallas_call(
        body,
        out_shape=out_shape,
        in_specs=in_specs,
        scratch_shapes=list(scratch),
        compiler_params=pltpu.CompilerParams(vmem_limit_bytes=48 << 20),
        cost_estimate=pl.CostEstimate(flops=flops, bytes_accessed=moved, transcendentals=0),
    )


def short_rows_body(grid_values, quad_weights, owner_map, legendre, diffusion):
    channels, half_total, cols = grid_values.shape
    groups = lax.axis_size("lat")
    pairs = groups // 2
    device = lax.axis_index("lat").astype(jnp.int32)
    waves = legendre.shape[1]
    lat_total = legendre.shape[2]
    slots = legendre.shape[0] // 2
    blocks = half_total // SUB
    points = cols * groups
    lines = cols * SUB
    whole = pl.BlockSpec(memory_space=pltpu.VMEM)
    shape = jax.ShapeDtypeStruct
    with jax.named_scope("pack"):
        mine = kernel_call(pack_kernel, shape((pairs, lines, LANES), BF16), [whole])(
            jnp.transpose(grid_values, (2, 0, 1))
        )
    same_core = [[2 * chip + core for chip in range(pairs)] for core in range(2)]
    partner = [(i, i ^ 1) for i in range(groups)]
    with jax.named_scope("gather"):
        own = lax.all_to_all(mine, "lat", split_axis=0, concat_axis=0, tiled=True, axis_index_groups=same_core)
    rates = jnp.pad(jnp.tile(jnp.repeat(diffusion, LEVELS), 2), (0, LANES - 2 * channels))[None, :]
    with jax.named_scope("tables"):
        tt, tr, wave, scale, factor = kernel_call(
            functools.partial(table_kernel, half_total, cols, waves),
            (
                shape((blocks, points, 4 * LANES), BF16),
                shape((blocks, 4 * LANES, points), BF16),
                shape((slots, LANES), F32),
                shape((2 * blocks, SUB, LANES), F32),
                shape((waves, LANES), F32),
            ),
            [pl.BlockSpec(memory_space=pltpu.SMEM), whole, whole, whole],
            [pltpu.VMEM((points, LANES), F32)],
            moved=8 << 20,
            flops=20 << 20,
        )(device[None], owner_map[None, :], quad_weights[None, :], rates)
    with jax.named_scope("swap"):
        other = lax.ppermute(own, "lat", partner)
    with jax.named_scope("transform"):
        sums = pl.pallas_call(
            main_kernel,
            grid=(1,),
            out_shape=shape((2, pairs, lines, LANES), BF16),
            in_specs=[whole] * 7 + [pl.BlockSpec((slots, waves, lat_total), lambda i: (0, 0, 0))],
            out_specs=whole,
            scratch_shapes=[
                pltpu.VMEM((points * SUB, LANES), F32),
                pltpu.VMEM((lat_total * slots, LANES), F32),
                pltpu.VMEM((lat_total * slots, LANES), F32),
            ],
            compiler_params=pltpu.CompilerParams(vmem_limit_bytes=48 << 20),
        )(own, other, tt, tr, wave, scale, factor, legendre)
    with jax.named_scope("join"):
        joined = (sums[0].astype(F32) + lax.ppermute(sums[1], "lat", partner).astype(F32)).astype(BF16)
    with jax.named_scope("scatter"):
        ready = lax.all_to_all(joined, "lat", split_axis=0, concat_axis=0, tiled=True, axis_index_groups=same_core)
    with jax.named_scope("unpack"):
        out = kernel_call(unpack_kernel, shape((cols, channels, half_total), BF16), [whole])(ready)
    return jnp.transpose(out, (1, 2, 0))


def body(grid_values, quad_weights, owner_map, legendre, diffusion):
    channels, half_total, cols = grid_values.shape
    slots, waves, lat_total = legendre.shape
    groups = lax.axis_size("lat")
    longest = 20 + 4 * (half_total - 1)
    short = (
        longest <= waves
        and groups % 2 == 0
        and half_total % groups == 0
        and half_total // groups * 2 == SUB
        and channels * SUB == LANES
        and channels * half_total == SUB * LANES
        and slots * SUB == 2 * LANES
        and lat_total == LANES
        and cols * groups % 16 == 0
    )
    if short:
        return short_rows_body(grid_values, quad_weights, owner_map, legendre, diffusion)
    return any_rows_body(grid_values, quad_weights, owner_map, legendre, diffusion)


def solution(mesh):
    return jax.shard_map(
        body,
        mesh=mesh,
        in_specs=(P("grp", None, "lat"), P(), P(), P("lat", None, None), P()),
        out_specs=P("grp", None, "lat"),
        check_vma=False,
    )
```

```python
import functools
import math

import jax
import jax.numpy as jnp
from jax import lax
from jax.experimental import pallas as pl
from jax.experimental.pallas import tpu as pltpu
from jax.sharding import PartitionSpec as P

LEVELS = 4


TWO_PI = 2.0 * math.pi


def pair_rows(lat_total):
    half = lat_total // 2
    quarter = lat_total // 4
    pair_ids = jnp.arange(half, dtype=jnp.int32)
    north = pair_ids < quarter
    shifted = pair_ids - quarter
    first = jnp.where(north, pair_ids, half + shifted)
    second = jnp.where(north, half - 1 - pair_ids, lat_total - 1 - shifted)
    return (first, second)


def row_length(lat_ids, lat_total):
    return 20 + 4 * jnp.minimum(lat_ids, lat_total - 1 - lat_ids)


def trig_table(length, offset, col_count, wave_ids):
    col_ids = jnp.arange(col_count, dtype=jnp.int32)
    local = col_ids - offset
    phases = local[:, None] * wave_ids[None, :] % length
    angles = phases.astype(jnp.float32) / length.astype(jnp.float32) * TWO_PI
    usable = (local[:, None] >= 0) & (local[:, None] < length) & (2 * wave_ids[None, :] < length)
    cos_part = jnp.where(usable, jnp.cos(angles), 0.0).astype(jnp.bfloat16)
    sin_part = jnp.where(usable, jnp.sin(angles), 0.0).astype(jnp.bfloat16)
    return jnp.concatenate([cos_part, sin_part], axis=1)


def any_rows_body(grid_values, quad_weights, owner_map, legendre, diffusion):
    channels, half_total, col_dev = grid_values.shape
    groups = lax.axis_size("lat")
    device = lax.axis_index("lat")
    half_dev = half_total // groups
    lat_total = 2 * half_total
    row_width = col_dev * groups
    owned_slots = legendre.shape[0]
    wave_count = legendre.shape[1]
    wave_ids = jnp.arange(wave_count, dtype=jnp.int32)
    slot_order = jnp.argsort(owner_map, stable=True)
    inverse_order = jnp.argsort(slot_order)
    my_waves = lax.dynamic_slice_in_dim(slot_order, device * owned_slots, owned_slots)
    contract = (((0,), (1,)), ((), ()))
    first, second = pair_rows(lat_total)
    my_first = lax.dynamic_slice_in_dim(first, device * half_dev, half_dev)
    my_second = lax.dynamic_slice_in_dim(second, device * half_dev, half_dev)
    first_len = row_length(my_first, lat_total)
    second_len = row_length(my_second, lat_total)
    first_weight = jnp.take(quad_weights, my_first)
    second_weight = jnp.take(quad_weights, my_second)

    def pair_tables(packed):
        len_a, len_b = packed
        return jnp.concatenate(
            [
                trig_table(len_a, 0, row_width, wave_ids),
                trig_table(len_b, len_a, row_width, wave_ids),
            ],
            axis=1,
        )

    all_tables = lax.map(pair_tables, (first_len, second_len))

    def forward_pair(row_data, tables):
        totals = lax.dot_general(tables, row_data, contract, preferred_element_type=jnp.float32)
        return (totals[: 2 * wave_count], totals[2 * wave_count :])

    def inverse_pair(coeffs_a, coeffs_b, tables):
        joined = jnp.concatenate([coeffs_a, coeffs_b], axis=0)
        return lax.dot_general(joined, tables, contract, preferred_element_type=jnp.float32).astype(
            jnp.bfloat16
        )

    def scaled(totals, weight, length):
        row_scale = weight / length.astype(jnp.float32)
        return jnp.concatenate(
            [totals[:wave_count] * row_scale, totals[wave_count:] * -row_scale], axis=0
        ).astype(jnp.bfloat16)

    def forward_one_pair(packed):
        row_data, tables, len_a, len_b, weight_a, weight_b = packed
        totals_a, totals_b = forward_pair(row_data, tables)
        return jnp.stack([scaled(totals_a, weight_a, len_a), scaled(totals_b, weight_b, len_b)])

    per_pair = lax.map(
        forward_one_pair,
        (
            jnp.moveaxis(
                lax.all_to_all(grid_values, "lat", split_axis=1, concat_axis=2, tiled=True), 1, 0
            ),
            all_tables,
            first_len,
            second_len,
            first_weight,
            second_weight,
        ),
    )
    per_lat = per_pair.transpose(1, 0, 2, 3).reshape(2 * half_dev, 2, wave_count, -1)
    fourier = per_lat.transpose(2, 1, 3, 0)
    picked = fourier[slot_order]
    rates = jnp.repeat(diffusion, LEVELS)
    degree = jnp.arange(wave_count, dtype=jnp.int32)
    ladder = (degree * (degree + 1)).astype(jnp.float32)
    factor = 1.0 / (1.0 + rates[:, None] * (ladder[None, :] / float(wave_count * (wave_count - 1))))
    damping = jnp.where((degree[None, :] >= my_waves[:, None])[:, None, :], factor[None, :, :], 0.0)
    spectral = jnp.einsum(
        "snl,spcl->spcn",
        legendre,
        lax.all_to_all(picked, "lat", split_axis=0, concat_axis=3, tiled=True),
        preferred_element_type=jnp.float32,
    )
    filtered = (spectral * damping[:, None, :, :]).astype(jnp.bfloat16)
    back = jnp.einsum("snl,spcn->spcl", legendre, filtered, preferred_element_type=jnp.float32)
    returned = back.astype(jnp.bfloat16)
    double = jnp.where(wave_ids == 0, 1.0, 2.0).astype(jnp.bfloat16)
    by_wave = lax.all_to_all(returned, "lat", split_axis=3, concat_axis=0, tiled=True)[
        inverse_order
    ]
    real_part = by_wave[:, 0] * double[:, None, None]
    imag_part = -(by_wave[:, 1] * double[:, None, None])
    stacked = jnp.concatenate([real_part, imag_part], axis=0)

    def backward_one_pair(packed):
        coeffs_a, coeffs_b, tables, len_a, len_b = packed
        return inverse_pair(coeffs_a, coeffs_b, tables)

    per_pair = lax.map(
        backward_one_pair,
        (
            jnp.moveaxis(stacked[:, :, :half_dev], 2, 0),
            jnp.moveaxis(stacked[:, :, half_dev:], 2, 0),
            all_tables,
            first_len,
            second_len,
        ),
    )
    rows_out = jnp.moveaxis(per_pair, 0, 1)
    return lax.all_to_all(rows_out, "lat", split_axis=2, concat_axis=1, tiled=True)


SIN_POLY = (3.141592640130707, -5.1677100835078775, 2.550077523214437, -0.5982912856197345, 0.07765766030450941)
COS_POLY = (0.9999999532476085, -4.934792830619644, 4.058411352862619, -1.3318765680811142, 0.2196896110983216)
LANES = 128
SUB = 8
F32 = jnp.float32
BF16 = jnp.bfloat16


def horner(poly, u):
    total = poly[-1]
    for term in poly[-2::-1]:
        total = total * u + term
    return total


def iota(shape, axis):
    return lax.broadcasted_iota(jnp.int32, shape, axis)


def swap_blocks(v):
    sub = iota(v.shape, 1)
    lane = iota(v.shape, 2)
    for bit in range(3):
        step = 1 << bit
        row_bit = (sub >> bit) & 1
        lane_bit = (lane >> (3 + bit)) & 1
        up = pltpu.roll(pltpu.roll(v, SUB - step, 1), SUB * step, 2)
        down = pltpu.roll(pltpu.roll(v, step, 1), LANES - SUB * step, 2)
        v = jnp.where(row_bit == lane_bit, v, jnp.where(row_bit == 0, up, down))
    return v


def pack_kernel(x_ref, o_ref):
    cols, channels, rows = x_ref.shape
    half = channels // 2
    x = x_ref[...].astype(F32)
    v = swap_blocks(jnp.concatenate([x[:, :half], x[:, half:]], axis=2))
    o_ref[...] = v.reshape(cols * SUB, LANES).astype(BF16)


def unpack_kernel(*refs):
    o_ref = refs[-1]
    cols, channels, rows = o_ref.shape
    half = channels // 2
    total = refs[0][...].astype(F32)
    for x_ref in refs[1:-1]:
        total = total + x_ref[...].astype(F32)
    v = swap_blocks(total.reshape(cols, SUB, LANES))
    o_ref[:, :half] = v[:, :, :rows].astype(BF16)
    o_ref[:, half:] = v[:, :, rows:].astype(BF16)


def join_kernel(x_ref, y_ref, o_ref):
    o_ref[...] = (x_ref[...].astype(F32) + y_ref[...].astype(F32)).astype(BF16)


def split_join_kernel(x_ref, y_ref, *o_refs):
    for i, o_ref in enumerate(o_refs):
        o_ref[...] = (x_ref[i].astype(F32) + y_ref[i].astype(F32)).astype(BF16)


def row_lengths(r, half_total):
    quarter = half_total // 2
    lat_total = 2 * half_total
    north = r < quarter
    first = jnp.where(north, r, half_total + r - quarter)
    second = jnp.where(north, half_total - 1 - r, lat_total - 1 - (r - quarter))
    return row_length(first, lat_total), row_length(second, lat_total)


def table_kernel(half_total, cols, waves, device_ref, owner_ref, tt_ref, wave_ref, jf_ref):
    points = tt_ref.shape[1]
    slots = wave_ref.shape[0]
    line = points // (4 * cols)
    device = device_ref[0]
    low = waves // 2
    owned = jnp.where(owner_ref[:, :low] == device, 1.0, 0.0)
    owned = jnp.broadcast_to(owned, (LANES, low)).T
    below = jnp.where(iota((low, low), 1) <= iota((low, low), 0), 1.0, 0.0).astype(BF16)
    count = jnp.dot(below, owned.astype(BF16), preferred_element_type=F32)
    wave_id = iota((low, LANES), 0).astype(F32)
    lane_slot = (iota((low, LANES), 1) % slots).astype(F32)
    hit = (owned > 0.5) & (count - 1.0 == lane_slot)
    wave = jnp.sum(jnp.where(hit, wave_id, 0.0), axis=0, keepdims=True)
    wave_ref[...] = jnp.broadcast_to(wave, (LANES, LANES)).T[:slots]
    place = iota((points, LANES), 0)
    origin = jnp.floor((place.astype(F32) + 0.5) * (1.0 / cols)).astype(jnp.int32)
    rest = place - origin * cols
    part = origin // line
    step = (origin - part * line) * 4 + (part & 1) * 2 + part // 2
    column = (device ^ step) * cols + rest
    jf_ref[...] = column.astype(F32)

    def block(t, carry):
        r = SUB * t + iota((1, LANES), 1) // slots
        len_a, len_b = row_lengths(r, half_total)
        len_a = len_a.astype(F32)
        len_b = len_b.astype(F32)
        inv_a = 1.0 / len_a
        inv_b = 1.0 / len_b
        end_a = jnp.where(2.0 * wave < len_a, len_a, 0.0)
        end_b = jnp.where(2.0 * wave < len_b, len_a + len_b, 0.0)
        for chunk in range(points // 16):
            span = slice(16 * chunk, 16 * chunk + 16)
            jf = jf_ref[span]
            in_a = jf < len_a
            length = jnp.where(in_a, len_a, len_b)
            inverse = jnp.where(in_a, inv_a, inv_b)
            phase = jnp.where(in_a, jf, jf - len_a) * wave
            turns = jnp.floor(phase * inverse + 0.5)
            part = (phase - turns * length) * inverse
            square = part * part
            half_sin = part * horner(SIN_POLY, square)
            half_cos = horner(COS_POLY, square)
            cos_part = 1.0 - 2.0 * (half_sin * half_sin)
            sin_part = 2.0 * (half_sin * half_cos)
            use_a = jf < end_a
            use_b = (jf < end_b) & jnp.logical_not(in_a)
            tt_ref[t, span, 0:LANES] = jnp.where(use_a, cos_part, 0.0).astype(BF16)
            tt_ref[t, span, LANES : 2 * LANES] = jnp.where(use_a, sin_part, 0.0).astype(BF16)
            tt_ref[t, span, 2 * LANES : 3 * LANES] = jnp.where(use_b, cos_part, 0.0).astype(BF16)
            tt_ref[t, span, 3 * LANES : 4 * LANES] = jnp.where(use_b, sin_part, 0.0).astype(BF16)
        return carry

    lax.fori_loop(0, half_total // SUB, block, 0)


def turn_kernel(half_total, tt_ref, weight_ref, rate_ref, tr_ref, scale_ref, factor_ref):
    lat_total = 2 * half_total
    waves = factor_ref.shape[0]

    def block(t, carry):
        for i in range(4):
            lanes = slice(i * LANES, (i + 1) * LANES)
            tr_ref[t, lanes, :] = tt_ref[t, :, lanes].T
        return carry

    lax.fori_loop(0, half_total // SUB, block, 0)
    weight = jnp.broadcast_to(weight_ref[...], (LANES, lat_total)).T
    scale = weight / row_length(iota((lat_total, LANES), 0), lat_total).astype(F32)
    keep = iota((SUB, LANES), 1) % SUB == iota((SUB, LANES), 0)
    quarter = half_total // 2
    for t in range(half_total // SUB):
        r = SUB * t
        if r < quarter:
            first, second = r, half_total - 1 - r
        else:
            first, second = half_total + r - quarter, lat_total - 1 - (r - quarter)
        under = scale[second - SUB + 1 : second + 1]
        under = jnp.concatenate([under[SUB - 1 - i : SUB - i] for i in range(SUB)], axis=0)
        scale_ref[2 * t] = jnp.where(keep, scale[first : first + SUB], 0.0)
        scale_ref[2 * t + 1] = jnp.where(keep, under, 0.0)
    fields = rate_ref.shape[1]
    field = iota((1, LANES), 1) % (LANES // SUB) // LEVELS
    rate = jnp.zeros((1, LANES), F32)
    for i in range(fields):
        rate = jnp.where(field == i, rate_ref[:, i : i + 1], rate)
    degree = iota((waves, LANES), 0)
    ladder = (degree * (degree + 1)).astype(F32) / float(waves * (waves - 1))
    factor_ref[...] = 1.0 / (1.0 + rate * ladder)


def main_kernel(
    x0_ref, x1_ref, x2_ref, x3_ref, tt_ref, tr_ref, wave_ref, scale_ref, factor_ref, leg_ref, o0_ref, o1_ref, o2_ref, o3_ref, z_ref, at_ref, bt_ref
):
    blocks, points, _ = tt_ref.shape
    slots, waves, lat_total = leg_ref.shape
    line, lines, _ = x0_ref.shape
    for i, x_ref in enumerate((x0_ref, x1_ref, x2_ref, x3_ref)):
        for j in range(line):
            z_ref[(i * line + j) * lines : (i * line + j + 1) * lines] = x_ref[j].astype(F32)
    row2 = iota((2 * LANES, LANES), 0)
    col2 = iota((2 * LANES, LANES), 1)
    gather = jnp.where(row2 // SUB == col2, jnp.where(row2 < LANES, 1.0, -1.0), 0.0).astype(BF16)
    row3 = iota((LANES, 2 * LANES), 0)
    col3 = iota((LANES, 2 * LANES), 1)
    spread = jnp.where(col3 // SUB == row3, jnp.where(col3 < LANES, 1.0, -1.0), 0.0).astype(BF16)
    slab = SUB * slots // 2

    def forward(t, carry):
        z = z_ref[pl.ds(t, points, stride=SUB), :].astype(BF16)
        d = jnp.dot(tr_ref[t], z, preferred_element_type=F32)
        for h in range(2):
            parts = []
            for p in range(2):
                base = (2 * h + p) * LANES
                rows = [
                    d[base + i * slots : base + (i + 1) * slots] * scale_ref[2 * t + h, i : i + 1, :]
                    for i in range(SUB)
                ]
                parts.append(jnp.concatenate(rows, axis=0).astype(BF16))
            a = jnp.dot(jnp.concatenate(parts, axis=1), gather, preferred_element_type=F32)
            for i in range(2):
                at_ref[pl.ds(pl.multiple_of((2 * t + i) * LANES + h * slab, SUB), slab), :] = a[i * slab : (i + 1) * slab]
        return carry

    lax.fori_loop(0, blocks, forward, 0, unroll=8)
    degree = iota((waves, LANES), 0).astype(F32)

    def slot(s, carry):
        f = at_ref[pl.ds(s, lat_total, stride=slots), :].astype(BF16)
        table = leg_ref[s]
        spectral = jnp.dot(table, f, preferred_element_type=F32)
        wave = wave_ref[pl.ds(s, 1), :]
        kept = jnp.where(degree >= wave, spectral * factor_ref[...], 0.0).astype(BF16)
        back = lax.dot_general(table, kept, (((0,), (0,)), ((), ())), preferred_element_type=F32)
        back = back.astype(BF16).astype(F32) * jnp.where(wave == 0.0, 1.0, 2.0)
        bt_ref[pl.ds(s, lat_total, stride=slots), :] = back
        return carry

    lax.fori_loop(0, slots, slot, 0, unroll=8)
    keep = (iota((LANES, 2 * LANES), 1) % SUB) == iota((LANES, 2 * LANES), 0) // slots

    def inverse(t, carry):
        rhs = []
        for h in range(2):
            b = jnp.concatenate(
                [bt_ref[pl.ds(pl.multiple_of((2 * t + i) * LANES + h * slab, SUB), slab), :] for i in range(2)], axis=0
            ).astype(BF16)
            wide = jnp.dot(b, spread, preferred_element_type=F32)
            wide = jnp.where(keep, wide, 0.0).astype(BF16)
            rhs.append(wide[:, :LANES])
            rhs.append(wide[:, LANES:])
        out = jnp.dot(tt_ref[t], jnp.concatenate(rhs, axis=0), preferred_element_type=F32)
        z_ref[pl.ds(t, points, stride=SUB), :] = out
        return carry

    lax.fori_loop(0, blocks, inverse, 0, unroll=4)
    for i, o_ref in enumerate((o0_ref, o1_ref, o2_ref, o3_ref)):
        for j in range(line):
            o_ref[j] = z_ref[(i * line + j) * lines : (i * line + j + 1) * lines].astype(BF16)


def kernel_call(body, out_shape, in_specs, scratch=(), flops=0, moved=0):
    return pl.pallas_call(
        body,
        out_shape=out_shape,
        in_specs=in_specs,
        scratch_shapes=list(scratch),
        compiler_params=pltpu.CompilerParams(vmem_limit_bytes=12 << 20),
        cost_estimate=pl.CostEstimate(flops=flops, bytes_accessed=moved, transcendentals=0),
    )


def transform_call(parts, tt, tr, wave, scale, factor, legendre):
    slots = wave.shape[0]
    waves, lat_total = legendre.shape[1:]
    line, lines, _ = parts[0].shape
    whole = pl.BlockSpec(memory_space=pltpu.VMEM)
    return pl.pallas_call(
        main_kernel,
        out_shape=[jax.ShapeDtypeStruct((line, lines, LANES), BF16)] * 4,
        in_specs=[whole] * 10,
        out_specs=[whole] * 4,
        scratch_shapes=[
            pltpu.VMEM((4 * line * lines, LANES), F32),
            pltpu.VMEM((lat_total * slots, LANES), F32),
            pltpu.VMEM((lat_total * slots, LANES), F32),
        ],
        compiler_params=pltpu.CompilerParams(vmem_limit_bytes=16 << 20),
    )(*parts, tt, tr, wave, scale, factor, legendre)


def short_rows_body(grid_values, quad_weights, owner_map, legendre, diffusion):
    channels, half_total, cols = grid_values.shape
    groups = lax.axis_size("lat")
    line = groups // 4
    device = lax.axis_index("lat").astype(jnp.int32)
    waves = legendre.shape[1]
    lat_total = legendre.shape[2]
    slots = legendre.shape[0] // 2
    blocks = half_total // SUB
    points = cols * groups
    lines = cols * SUB
    whole = pl.BlockSpec(memory_space=pltpu.VMEM)
    shape = jax.ShapeDtypeStruct
    with jax.named_scope("pack"):
        mine = kernel_call(pack_kernel, shape((lines, LANES), BF16), [whole])(jnp.transpose(grid_values, (2, 0, 1)))

    def across(x, step):
        return lax.ppermute(x, "lat", [(i, i ^ step) for i in range(groups)])

    with jax.named_scope("gather_line"):
        arrived = [across(mine, 4 * i) for i in range(line - 1, 0, -1)]
    with jax.named_scope("tables"):
        tt, wave = kernel_call(
            functools.partial(table_kernel, half_total, cols, waves),
            (shape((blocks, points, 4 * LANES), BF16), shape((slots, LANES), F32)),
            [pl.BlockSpec(memory_space=pltpu.SMEM), whole],
            [pltpu.VMEM((points, LANES), F32)],
            flops=12 << 20,
            moved=3 << 20,
        )(device[None], owner_map[None, :])
        half_legendre = legendre[:slots]
        arrived, tt, wave, half_legendre = lax.optimization_barrier((arrived, tt, wave, half_legendre))
    with jax.named_scope("gather_line"):
        p0 = jnp.stack([mine] + arrived[::-1])
    with jax.named_scope("gather_plane"):
        p1 = across(p0, 2)
        tr, scale, factor = kernel_call(
            functools.partial(turn_kernel, half_total),
            (
                shape((blocks, 4 * LANES, points), BF16),
                shape((2 * blocks, SUB, LANES), F32),
                shape((waves, LANES), F32),
            ),
            [whole, whole, whole],
            flops=12 << 20,
            moved=6 << 20,
        )(tt, quad_weights[None, :], diffusion[None, :])
        p1, tr, scale, factor = lax.optimization_barrier((p1, tr, scale, factor))
        p2 = across(p0, 1)
        p3 = across(p1, 1)
    with jax.named_scope("transform"):
        s0, s1, s2, s3 = transform_call((p0, p1, p2, p3), tt, tr, wave, scale, factor, half_legendre)
    block = shape((line, lines, LANES), BF16)
    with jax.named_scope("sum_cores"):
        far = kernel_call(join_kernel, block, [whole] * 2)(s1, across(s3, 1))
        near = kernel_call(join_kernel, block, [whole] * 2)(s0, across(s2, 1))
    with jax.named_scope("sum_plane"):
        ends = kernel_call(split_join_kernel, [shape((lines, LANES), BF16)] * line, [whole] * 2)(near, across(far, 2))
    with jax.named_scope("sum_line"):
        ready = [ends[0]] + [across(ends[i], 4 * i) for i in range(line - 1, 0, -1)]
    with jax.named_scope("unpack"):
        out = kernel_call(unpack_kernel, shape((cols, channels, half_total), BF16), [whole] * line)(*ready)
    return jnp.transpose(out, (1, 2, 0))


def body(grid_values, quad_weights, owner_map, legendre, diffusion):
    channels, half_total, cols = grid_values.shape
    slots, waves, lat_total = legendre.shape
    groups = lax.axis_size("lat")
    longest = 20 + 4 * (half_total - 1)
    short = (
        longest <= waves
        and groups >= 8
        and groups & (groups - 1) == 0
        and half_total % groups == 0
        and half_total // groups * 2 == SUB
        and channels * SUB == LANES
        and channels * half_total == SUB * LANES
        and slots * SUB == 2 * LANES
        and lat_total == LANES
        and cols * groups % 16 == 0
    )
    if short:
        return short_rows_body(grid_values, quad_weights, owner_map, legendre, diffusion)
    return any_rows_body(grid_values, quad_weights, owner_map, legendre, diffusion)


def solution(mesh):
    return jax.shard_map(
        body,
        mesh=mesh,
        in_specs=(P("grp", None, "lat"), P(), P(), P("lat", None, None), P()),
        out_specs=P("grp", None, "lat"),
        check_vma=False,
    )
```

```python
import functools
import math

import jax
import jax.numpy as jnp
from jax import lax
from jax.experimental import pallas as pl
from jax.experimental.pallas import tpu as pltpu
from jax.sharding import PartitionSpec as P

LEVELS = 4


TWO_PI = 2.0 * math.pi


def pair_rows(lat_total):
    half = lat_total // 2
    quarter = lat_total // 4
    pair_ids = jnp.arange(half, dtype=jnp.int32)
    north = pair_ids < quarter
    shifted = pair_ids - quarter
    first = jnp.where(north, pair_ids, half + shifted)
    second = jnp.where(north, half - 1 - pair_ids, lat_total - 1 - shifted)
    return (first, second)


def row_length(lat_ids, lat_total):
    return 20 + 4 * jnp.minimum(lat_ids, lat_total - 1 - lat_ids)


def trig_table(length, offset, col_count, wave_ids):
    col_ids = jnp.arange(col_count, dtype=jnp.int32)
    local = col_ids - offset
    phases = local[:, None] * wave_ids[None, :] % length
    angles = phases.astype(jnp.float32) / length.astype(jnp.float32) * TWO_PI
    usable = (local[:, None] >= 0) & (local[:, None] < length) & (2 * wave_ids[None, :] < length)
    cos_part = jnp.where(usable, jnp.cos(angles), 0.0).astype(jnp.bfloat16)
    sin_part = jnp.where(usable, jnp.sin(angles), 0.0).astype(jnp.bfloat16)
    return jnp.concatenate([cos_part, sin_part], axis=1)


def any_rows_body(grid_values, quad_weights, owner_map, legendre, diffusion):
    channels, half_total, col_dev = grid_values.shape
    groups = lax.axis_size("lat")
    device = lax.axis_index("lat")
    half_dev = half_total // groups
    lat_total = 2 * half_total
    row_width = col_dev * groups
    owned_slots = legendre.shape[0]
    wave_count = legendre.shape[1]
    wave_ids = jnp.arange(wave_count, dtype=jnp.int32)
    slot_order = jnp.argsort(owner_map, stable=True)
    inverse_order = jnp.argsort(slot_order)
    my_waves = lax.dynamic_slice_in_dim(slot_order, device * owned_slots, owned_slots)
    contract = (((0,), (1,)), ((), ()))
    first, second = pair_rows(lat_total)
    my_first = lax.dynamic_slice_in_dim(first, device * half_dev, half_dev)
    my_second = lax.dynamic_slice_in_dim(second, device * half_dev, half_dev)
    first_len = row_length(my_first, lat_total)
    second_len = row_length(my_second, lat_total)
    first_weight = jnp.take(quad_weights, my_first)
    second_weight = jnp.take(quad_weights, my_second)

    def pair_tables(packed):
        len_a, len_b = packed
        return jnp.concatenate(
            [
                trig_table(len_a, 0, row_width, wave_ids),
                trig_table(len_b, len_a, row_width, wave_ids),
            ],
            axis=1,
        )

    all_tables = lax.map(pair_tables, (first_len, second_len))

    def forward_pair(row_data, tables):
        totals = lax.dot_general(tables, row_data, contract, preferred_element_type=jnp.float32)
        return (totals[: 2 * wave_count], totals[2 * wave_count :])

    def inverse_pair(coeffs_a, coeffs_b, tables):
        joined = jnp.concatenate([coeffs_a, coeffs_b], axis=0)
        return lax.dot_general(joined, tables, contract, preferred_element_type=jnp.float32).astype(
            jnp.bfloat16
        )

    def scaled(totals, weight, length):
        row_scale = weight / length.astype(jnp.float32)
        return jnp.concatenate(
            [totals[:wave_count] * row_scale, totals[wave_count:] * -row_scale], axis=0
        ).astype(jnp.bfloat16)

    def forward_one_pair(packed):
        row_data, tables, len_a, len_b, weight_a, weight_b = packed
        totals_a, totals_b = forward_pair(row_data, tables)
        return jnp.stack([scaled(totals_a, weight_a, len_a), scaled(totals_b, weight_b, len_b)])

    per_pair = lax.map(
        forward_one_pair,
        (
            jnp.moveaxis(
                lax.all_to_all(grid_values, "lat", split_axis=1, concat_axis=2, tiled=True), 1, 0
            ),
            all_tables,
            first_len,
            second_len,
            first_weight,
            second_weight,
        ),
    )
    per_lat = per_pair.transpose(1, 0, 2, 3).reshape(2 * half_dev, 2, wave_count, -1)
    fourier = per_lat.transpose(2, 1, 3, 0)
    picked = fourier[slot_order]
    rates = jnp.repeat(diffusion, LEVELS)
    degree = jnp.arange(wave_count, dtype=jnp.int32)
    ladder = (degree * (degree + 1)).astype(jnp.float32)
    factor = 1.0 / (1.0 + rates[:, None] * (ladder[None, :] / float(wave_count * (wave_count - 1))))
    damping = jnp.where((degree[None, :] >= my_waves[:, None])[:, None, :], factor[None, :, :], 0.0)
    spectral = jnp.einsum(
        "snl,spcl->spcn",
        legendre,
        lax.all_to_all(picked, "lat", split_axis=0, concat_axis=3, tiled=True),
        preferred_element_type=jnp.float32,
    )
    filtered = (spectral * damping[:, None, :, :]).astype(jnp.bfloat16)
    back = jnp.einsum("snl,spcn->spcl", legendre, filtered, preferred_element_type=jnp.float32)
    returned = back.astype(jnp.bfloat16)
    double = jnp.where(wave_ids == 0, 1.0, 2.0).astype(jnp.bfloat16)
    by_wave = lax.all_to_all(returned, "lat", split_axis=3, concat_axis=0, tiled=True)[
        inverse_order
    ]
    real_part = by_wave[:, 0] * double[:, None, None]
    imag_part = -(by_wave[:, 1] * double[:, None, None])
    stacked = jnp.concatenate([real_part, imag_part], axis=0)

    def backward_one_pair(packed):
        coeffs_a, coeffs_b, tables, len_a, len_b = packed
        return inverse_pair(coeffs_a, coeffs_b, tables)

    per_pair = lax.map(
        backward_one_pair,
        (
            jnp.moveaxis(stacked[:, :, :half_dev], 2, 0),
            jnp.moveaxis(stacked[:, :, half_dev:], 2, 0),
            all_tables,
            first_len,
            second_len,
        ),
    )
    rows_out = jnp.moveaxis(per_pair, 0, 1)
    return lax.all_to_all(rows_out, "lat", split_axis=2, concat_axis=1, tiled=True)


SIN_POLY = (3.141592640130707, -5.1677100835078775, 2.550077523214437, -0.5982912856197345, 0.07765766030450941)
COS_POLY = (0.9999999532476085, -4.934792830619644, 4.058411352862619, -1.3318765680811142, 0.2196896110983216)
LANES = 128
SUB = 8
HOPS = (0, 1, 2, 3)
SEND_ORDER = (3, 2)
GATHER_ORDER = (1, 2, 3)
F32 = jnp.float32
BF16 = jnp.bfloat16


def horner(poly, u):
    total = poly[-1]
    for term in poly[-2::-1]:
        total = total * u + term
    return total


def iota(shape, axis):
    return lax.broadcasted_iota(jnp.int32, shape, axis)


def swap_blocks(v):
    sub = iota(v.shape, 1)
    lane = iota(v.shape, 2)
    for bit in range(3):
        step = 1 << bit
        row_bit = (sub >> bit) & 1
        lane_bit = (lane >> (3 + bit)) & 1
        up = pltpu.roll(pltpu.roll(v, SUB - step, 1), SUB * step, 2)
        down = pltpu.roll(pltpu.roll(v, step, 1), LANES - SUB * step, 2)
        v = jnp.where(row_bit == lane_bit, v, jnp.where(row_bit == 0, up, down))
    return v


def pack_kernel(x_ref, o_ref):
    cols, channels, rows = x_ref.shape
    half = channels // 2
    x = x_ref[...].astype(F32)
    v = swap_blocks(jnp.concatenate([x[:, :half], x[:, half:]], axis=2))
    o_ref[...] = v.reshape(cols * SUB, LANES).astype(BF16)


def unpack_kernel(*refs):
    o_ref = refs[-1]
    cols, channels, rows = o_ref.shape
    half = channels // 2
    total = refs[0][...].astype(F32)
    for x_ref in refs[1:-1]:
        total = total + x_ref[...].astype(F32)
    v = swap_blocks(total.reshape(cols, SUB, LANES))
    o_ref[:, :half] = v[:, :, :rows].astype(BF16)
    o_ref[:, half:] = v[:, :, rows:].astype(BF16)


def join_kernel(x_ref, y_ref, *o_refs):
    start = 0
    for o_ref in o_refs:
        stop = start + o_ref.shape[0]
        o_ref[...] = (x_ref[start:stop].astype(F32) + y_ref[start:stop].astype(F32)).astype(BF16)
        start = stop


def end_kernel(start, x_ref, y_ref, z_ref, *o_refs):
    for i, o_ref in enumerate(o_refs):
        total = x_ref[start + i].astype(F32) + y_ref[start + i].astype(F32) + z_ref[i].astype(F32)
        o_ref[...] = total.astype(BF16)


def row_lengths(r, half_total):
    quarter = half_total // 2
    lat_total = 2 * half_total
    north = r < quarter
    first = jnp.where(north, r, half_total + r - quarter)
    second = jnp.where(north, half_total - 1 - r, lat_total - 1 - (r - quarter))
    return row_length(first, lat_total), row_length(second, lat_total)


def table_kernel(half_total, cols, waves, device_ref, owner_ref, tt_ref, wave_ref, jf_ref):
    points = tt_ref.shape[1]
    slots = wave_ref.shape[0]
    line = points // (4 * cols)
    device = device_ref[0]
    low = waves // 2
    owned = jnp.where(owner_ref[:, :low] == device, 1.0, 0.0)
    owned = jnp.broadcast_to(owned, (LANES, low)).T
    below = jnp.where(iota((low, low), 1) <= iota((low, low), 0), 1.0, 0.0).astype(BF16)
    count = jnp.dot(below, owned.astype(BF16), preferred_element_type=F32)
    wave_id = iota((low, LANES), 0).astype(F32)
    lane_slot = (iota((low, LANES), 1) % slots).astype(F32)
    hit = (owned > 0.5) & (count - 1.0 == lane_slot)
    wave = jnp.sum(jnp.where(hit, wave_id, 0.0), axis=0, keepdims=True)
    wave_ref[...] = jnp.broadcast_to(wave, (LANES, LANES)).T[:slots]
    place = iota((points, LANES), 0)
    origin = jnp.floor((place.astype(F32) + 0.5) * (1.0 / cols)).astype(jnp.int32)
    rest = place - origin * cols
    part = origin // line
    line_id = origin - part * line
    part = jnp.where(part < 2, 2 * part + 1, 2 * part - 4)
    hop = sum(jnp.where(line_id == i, HOPS[i], 0) for i in range(1, line))
    step = hop * 4 + (part & 1) * 2 + part // 2
    column = (device ^ step) * cols + rest
    jf_ref[...] = column.astype(F32)

    def block(t, carry):
        r = SUB * t + iota((1, LANES), 1) // slots
        len_a, len_b = row_lengths(r, half_total)
        len_a = len_a.astype(F32)
        len_b = len_b.astype(F32)
        inv_a = 1.0 / len_a
        inv_b = 1.0 / len_b
        end_a = jnp.where(2.0 * wave < len_a, len_a, 0.0)
        end_b = jnp.where(2.0 * wave < len_b, len_a + len_b, 0.0)
        for chunk in range(points // 16):
            span = slice(16 * chunk, 16 * chunk + 16)
            jf = jf_ref[span]
            in_a = jf < len_a
            length = jnp.where(in_a, len_a, len_b)
            inverse = jnp.where(in_a, inv_a, inv_b)
            phase = jnp.where(in_a, jf, jf - len_a) * wave
            turns = jnp.floor(phase * inverse + 0.5)
            part = (phase - turns * length) * inverse
            square = part * part
            half_sin = part * horner(SIN_POLY, square)
            half_cos = horner(COS_POLY, square)
            cos_part = 1.0 - 2.0 * (half_sin * half_sin)
            sin_part = 2.0 * (half_sin * half_cos)
            use_a = jf < end_a
            use_b = (jf < end_b) & jnp.logical_not(in_a)
            tt_ref[t, span, 0:LANES] = jnp.where(use_a, cos_part, 0.0).astype(BF16)
            tt_ref[t, span, LANES : 2 * LANES] = jnp.where(use_a, sin_part, 0.0).astype(BF16)
            tt_ref[t, span, 2 * LANES : 3 * LANES] = jnp.where(use_b, cos_part, 0.0).astype(BF16)
            tt_ref[t, span, 3 * LANES : 4 * LANES] = jnp.where(use_b, sin_part, 0.0).astype(BF16)
        return carry

    lax.fori_loop(0, half_total // SUB, block, 0)


def turn_kernel(half_total, tt_ref, weight_ref, rate_ref, tr_ref, scale_ref, factor_ref):
    lat_total = 2 * half_total
    waves = factor_ref.shape[0]

    def block(t, carry):
        for i in range(4):
            lanes = slice(i * LANES, (i + 1) * LANES)
            tr_ref[t, lanes, :] = tt_ref[t, :, lanes].T
        return carry

    lax.fori_loop(0, half_total // SUB, block, 0)
    weight = jnp.broadcast_to(weight_ref[...], (LANES, lat_total)).T
    scale = weight / row_length(iota((lat_total, LANES), 0), lat_total).astype(F32)
    keep = iota((SUB, LANES), 1) % SUB == iota((SUB, LANES), 0)
    quarter = half_total // 2
    for t in range(half_total // SUB):
        r = SUB * t
        if r < quarter:
            first, second = r, half_total - 1 - r
        else:
            first, second = half_total + r - quarter, lat_total - 1 - (r - quarter)
        under = scale[second - SUB + 1 : second + 1]
        under = jnp.concatenate([under[SUB - 1 - i : SUB - i] for i in range(SUB)], axis=0)
        scale_ref[2 * t] = jnp.where(keep, scale[first : first + SUB], 0.0)
        scale_ref[2 * t + 1] = jnp.where(keep, under, 0.0)
    fields = rate_ref.shape[1]
    field = iota((1, LANES), 1) % (LANES // SUB) // LEVELS
    rate = jnp.zeros((1, LANES), F32)
    for i in range(fields):
        rate = jnp.where(field == i, rate_ref[:, i : i + 1], rate)
    degree = iota((waves, LANES), 0)
    ladder = (degree * (degree + 1)).astype(F32) / float(waves * (waves - 1))
    factor_ref[...] = 1.0 / (1.0 + rate * ladder)


def main_kernel(
    x0_ref, x1_ref, x2_ref, x3_ref, tt_ref, tr_ref, wave_ref, scale_ref, factor_ref, leg_ref, o1_ref, o3_ref, rhs_ref, z_ref, at_ref, bt_ref
):
    blocks, points, _ = tt_ref.shape
    slots, waves, lat_total = leg_ref.shape
    line, lines, _ = x0_ref.shape
    for i, x_ref in enumerate((x1_ref, x3_ref, x0_ref, x2_ref)):
        for j in range(line):
            z_ref[(i * line + j) * lines : (i * line + j + 1) * lines] = x_ref[j].astype(F32)
    row2 = iota((2 * LANES, LANES), 0)
    col2 = iota((2 * LANES, LANES), 1)
    gather = jnp.where(row2 // SUB == col2, jnp.where(row2 < LANES, 1.0, -1.0), 0.0).astype(BF16)
    row3 = iota((LANES, 2 * LANES), 0)
    col3 = iota((LANES, 2 * LANES), 1)
    spread = jnp.where(col3 // SUB == row3, jnp.where(col3 < LANES, 1.0, -1.0), 0.0).astype(BF16)
    slab = SUB * slots // 2

    def forward(t, carry):
        z = z_ref[pl.ds(t, points, stride=SUB), :].astype(BF16)
        d = jnp.dot(tr_ref[t], z, preferred_element_type=F32)
        for h in range(2):
            parts = []
            for p in range(2):
                base = (2 * h + p) * LANES
                rows = [
                    d[base + i * slots : base + (i + 1) * slots] * scale_ref[2 * t + h, i : i + 1, :]
                    for i in range(SUB)
                ]
                parts.append(jnp.concatenate(rows, axis=0).astype(BF16))
            a = jnp.dot(jnp.concatenate(parts, axis=1), gather, preferred_element_type=F32)
            for i in range(2):
                at_ref[pl.ds(pl.multiple_of((2 * t + i) * LANES + h * slab, SUB), slab), :] = a[i * slab : (i + 1) * slab]
        return carry

    lax.fori_loop(0, blocks, forward, 0, unroll=8)
    degree = iota((waves, LANES), 0).astype(F32)

    def slot(s, carry):
        f = at_ref[pl.ds(s, lat_total, stride=slots), :].astype(BF16)
        table = leg_ref[s]
        spectral = jnp.dot(table, f, preferred_element_type=F32)
        wave = wave_ref[pl.ds(s, 1), :]
        kept = jnp.where(degree >= wave, spectral * factor_ref[...], 0.0).astype(BF16)
        back = lax.dot_general(table, kept, (((0,), (0,)), ((), ())), preferred_element_type=F32)
        back = back.astype(BF16).astype(F32) * jnp.where(wave == 0.0, 1.0, 2.0)
        bt_ref[pl.ds(s, lat_total, stride=slots), :] = back
        return carry

    lax.fori_loop(0, slots, slot, 0, unroll=16)
    reach = -(points // 2) // 16 * -16
    keep = (iota((LANES, 2 * LANES), 1) % SUB) == iota((LANES, 2 * LANES), 0) // slots

    def inverse(t, carry):
        rhs = []
        for h in range(2):
            b = jnp.concatenate(
                [bt_ref[pl.ds(pl.multiple_of((2 * t + i) * LANES + h * slab, SUB), slab), :] for i in range(2)], axis=0
            ).astype(BF16)
            wide = jnp.dot(b, spread, preferred_element_type=F32)
            wide = jnp.where(keep, wide, 0.0).astype(BF16)
            rhs.append(wide[:, :LANES])
            rhs.append(wide[:, LANES:])
        rhs = jnp.concatenate(rhs, axis=0)
        rhs_ref[t] = rhs
        out = jnp.dot(tt_ref[t, :reach], rhs, preferred_element_type=F32)
        z_ref[pl.ds(t, points // 2, stride=SUB), :] = out[: points // 2]
        return carry

    lax.fori_loop(0, blocks, inverse, 0, unroll=8)
    for i, o_ref in enumerate((o1_ref, o3_ref)):
        for j in range(line):
            o_ref[j] = z_ref[(i * line + j) * lines : (i * line + j + 1) * lines].astype(BF16)


def near_kernel(tt_ref, rhs_ref, o0_ref, o2_ref, z_ref):
    blocks, points, _ = tt_ref.shape
    line, lines, _ = o0_ref.shape
    from_row = points // 2 // 16 * 16

    def inverse(t, carry):
        out = jnp.dot(tt_ref[t, from_row:], rhs_ref[t], preferred_element_type=F32)
        z_ref[pl.ds(t, points // 2, stride=SUB), :] = out[points // 2 - from_row :]
        return carry

    lax.fori_loop(0, blocks, inverse, 0, unroll=8)
    for i, o_ref in enumerate((o0_ref, o2_ref)):
        for j in range(line):
            o_ref[j] = z_ref[(i * line + j) * lines : (i * line + j + 1) * lines].astype(BF16)


def kernel_call(body, out_shape, in_specs, scratch=(), flops=0, moved=0):
    return pl.pallas_call(
        body,
        out_shape=out_shape,
        in_specs=in_specs,
        scratch_shapes=list(scratch),
        compiler_params=pltpu.CompilerParams(vmem_limit_bytes=12 << 20),
        cost_estimate=pl.CostEstimate(flops=flops, bytes_accessed=moved, transcendentals=0),
    )


def transform_call(parts, tt, tr, wave, scale, factor, legendre):
    slots = wave.shape[0]
    waves, lat_total = legendre.shape[1:]
    line, lines, _ = parts[0].shape
    whole = pl.BlockSpec(memory_space=pltpu.VMEM)
    return pl.pallas_call(
        main_kernel,
        out_shape=[jax.ShapeDtypeStruct((line, lines, LANES), BF16)] * 2
        + [jax.ShapeDtypeStruct(tt.shape[:1] + (4 * LANES, LANES), BF16)],
        in_specs=[whole] * 10,
        out_specs=[whole] * 3,
        scratch_shapes=[
            pltpu.VMEM((4 * line * lines, LANES), F32),
            pltpu.VMEM((lat_total * slots, LANES), F32),
            pltpu.VMEM((lat_total * slots, LANES), F32),
        ],
        compiler_params=pltpu.CompilerParams(vmem_limit_bytes=16 << 20),
    )(*parts, tt, tr, wave, scale, factor, legendre)


def short_rows_body(grid_values, quad_weights, owner_map, legendre, diffusion):
    channels, half_total, cols = grid_values.shape
    groups = lax.axis_size("lat")
    line = groups // 4
    device = lax.axis_index("lat").astype(jnp.int32)
    waves = legendre.shape[1]
    lat_total = legendre.shape[2]
    slots = legendre.shape[0] // 2
    blocks = half_total // SUB
    points = cols * groups
    lines = cols * SUB
    whole = pl.BlockSpec(memory_space=pltpu.VMEM)
    shape = jax.ShapeDtypeStruct
    with jax.named_scope("pack"):
        mine = kernel_call(pack_kernel, shape((lines, LANES), BF16), [whole])(jnp.transpose(grid_values, (2, 0, 1)))

    def across(x, step):
        return lax.ppermute(x, "lat", [(i, i ^ step) for i in range(groups)])

    with jax.named_scope("gather_line"):
        arrived = {hop: across(mine, 4 * hop) for hop in GATHER_ORDER}
        arrived = [arrived[hop] for hop in HOPS[1:]]
    with jax.named_scope("tables"):
        tt, wave = kernel_call(
            functools.partial(table_kernel, half_total, cols, waves),
            (shape((blocks, points, 4 * LANES), BF16), shape((slots, LANES), F32)),
            [pl.BlockSpec(memory_space=pltpu.SMEM), whole],
            [pltpu.VMEM((points, LANES), F32)],
            flops=12 << 20,
            moved=3 << 20,
        )(device[None], owner_map[None, :])
        arrived, tt, wave = lax.optimization_barrier((arrived, tt, wave))
    with jax.named_scope("gather_line"):
        p0 = jnp.stack([mine] + arrived)
    with jax.named_scope("gather_plane"):
        p1 = across(p0, 2)
        tr, scale, factor = kernel_call(
            functools.partial(turn_kernel, half_total),
            (
                shape((blocks, 4 * LANES, points), BF16),
                shape((2 * blocks, SUB, LANES), F32),
                shape((waves, LANES), F32),
            ),
            [whole, whole, whole],
            flops=12 << 20,
            moved=6 << 20,
        )(tt, quad_weights[None, :], diffusion[None, :])
        half_legendre = legendre[:slots]
        p1, tr, scale, factor, half_legendre = lax.optimization_barrier((p1, tr, scale, factor, half_legendre))
        p2 = across(p0, 1)
        p3 = across(p1, 1)
    with jax.named_scope("transform"):
        s1, s3, rhs = transform_call((p0, p1, p2, p3), tt, tr, wave, scale, factor, half_legendre)
    block = shape((line, lines, LANES), BF16)
    half_block = shape((line // 2, lines, LANES), BF16)
    with jax.named_scope("sum_cores"):
        r3 = across(s3, 1)
        s0, s2 = kernel_call(near_kernel, [block] * 2, [whole] * 2, [pltpu.VMEM((2 * line * lines, LANES), F32)])(tt, rhs)
        near, far = kernel_call(join_kernel, [half_block] * 2, [whole] * 2)(s1, r3)
        r2 = across(s2, 1)
    with jax.named_scope("sum_plane"):
        far = across(far, 2)
        near = across(near, 2)
    with jax.named_scope("sum_line"):
        one = [shape((lines, LANES), BF16)] * (line // 2)
        ends = kernel_call(functools.partial(end_kernel, line // 2), one, [whole] * 3)(s0, r2, far)
        ready = [across(ends[i - line // 2], 4 * HOPS[i]) for i in SEND_ORDER]
        ends = kernel_call(functools.partial(end_kernel, 0), one, [whole] * 3)(s0, r2, near)
        ready += [across(ends[i], 4 * HOPS[i]) for i in range(1, line // 2)] + [ends[0]]
    with jax.named_scope("unpack"):
        out = kernel_call(unpack_kernel, shape((cols, channels, half_total), BF16), [whole] * line)(*ready)
    return jnp.transpose(out, (1, 2, 0))


def body(grid_values, quad_weights, owner_map, legendre, diffusion):
    channels, half_total, cols = grid_values.shape
    slots, waves, lat_total = legendre.shape
    groups = lax.axis_size("lat")
    longest = 20 + 4 * (half_total - 1)
    short = (
        longest <= waves
        and groups >= 8
        and groups & (groups - 1) == 0
        and half_total % groups == 0
        and half_total // groups * 2 == SUB
        and groups == 4 * len(HOPS)
        and channels * SUB == LANES
        and channels * half_total == SUB * LANES
        and slots * SUB == 2 * LANES
        and lat_total == LANES
        and cols * groups % 16 == 0
    )
    if short:
        return short_rows_body(grid_values, quad_weights, owner_map, legendre, diffusion)
    return any_rows_body(grid_values, quad_weights, owner_map, legendre, diffusion)


def solution(mesh):
    return jax.shard_map(
        body,
        mesh=mesh,
        in_specs=(P("grp", None, "lat"), P(), P(), P("lat", None, None), P()),
        out_specs=P("grp", None, "lat"),
        check_vma=False,
    )
```

```python
import functools
import math

import jax
import jax.numpy as jnp
from jax import lax
from jax.experimental import pallas as pl
from jax.experimental.pallas import tpu as pltpu
from jax.sharding import PartitionSpec as P

LEVELS = 4


TWO_PI = 2.0 * math.pi


def pair_rows(lat_total):
    half = lat_total // 2
    quarter = lat_total // 4
    pair_ids = jnp.arange(half, dtype=jnp.int32)
    north = pair_ids < quarter
    shifted = pair_ids - quarter
    first = jnp.where(north, pair_ids, half + shifted)
    second = jnp.where(north, half - 1 - pair_ids, lat_total - 1 - shifted)
    return (first, second)


def row_length(lat_ids, lat_total):
    return 20 + 4 * jnp.minimum(lat_ids, lat_total - 1 - lat_ids)


def trig_table(length, offset, col_count, wave_ids):
    col_ids = jnp.arange(col_count, dtype=jnp.int32)
    local = col_ids - offset
    phases = local[:, None] * wave_ids[None, :] % length
    angles = phases.astype(jnp.float32) / length.astype(jnp.float32) * TWO_PI
    usable = (local[:, None] >= 0) & (local[:, None] < length) & (2 * wave_ids[None, :] < length)
    cos_part = jnp.where(usable, jnp.cos(angles), 0.0).astype(jnp.bfloat16)
    sin_part = jnp.where(usable, jnp.sin(angles), 0.0).astype(jnp.bfloat16)
    return jnp.concatenate([cos_part, sin_part], axis=1)


def any_rows_body(grid_values, quad_weights, owner_map, legendre, diffusion):
    channels, half_total, col_dev = grid_values.shape
    groups = lax.axis_size("lat")
    device = lax.axis_index("lat")
    half_dev = half_total // groups
    lat_total = 2 * half_total
    row_width = col_dev * groups
    owned_slots = legendre.shape[0]
    wave_count = legendre.shape[1]
    wave_ids = jnp.arange(wave_count, dtype=jnp.int32)
    slot_order = jnp.argsort(owner_map, stable=True)
    inverse_order = jnp.argsort(slot_order)
    my_waves = lax.dynamic_slice_in_dim(slot_order, device * owned_slots, owned_slots)
    contract = (((0,), (1,)), ((), ()))
    first, second = pair_rows(lat_total)
    my_first = lax.dynamic_slice_in_dim(first, device * half_dev, half_dev)
    my_second = lax.dynamic_slice_in_dim(second, device * half_dev, half_dev)
    first_len = row_length(my_first, lat_total)
    second_len = row_length(my_second, lat_total)
    first_weight = jnp.take(quad_weights, my_first)
    second_weight = jnp.take(quad_weights, my_second)

    def pair_tables(packed):
        len_a, len_b = packed
        return jnp.concatenate(
            [
                trig_table(len_a, 0, row_width, wave_ids),
                trig_table(len_b, len_a, row_width, wave_ids),
            ],
            axis=1,
        )

    all_tables = lax.map(pair_tables, (first_len, second_len))

    def forward_pair(row_data, tables):
        totals = lax.dot_general(tables, row_data, contract, preferred_element_type=jnp.float32)
        return (totals[: 2 * wave_count], totals[2 * wave_count :])

    def inverse_pair(coeffs_a, coeffs_b, tables):
        joined = jnp.concatenate([coeffs_a, coeffs_b], axis=0)
        return lax.dot_general(joined, tables, contract, preferred_element_type=jnp.float32).astype(
            jnp.bfloat16
        )

    def scaled(totals, weight, length):
        row_scale = weight / length.astype(jnp.float32)
        return jnp.concatenate(
            [totals[:wave_count] * row_scale, totals[wave_count:] * -row_scale], axis=0
        ).astype(jnp.bfloat16)

    def forward_one_pair(packed):
        row_data, tables, len_a, len_b, weight_a, weight_b = packed
        totals_a, totals_b = forward_pair(row_data, tables)
        return jnp.stack([scaled(totals_a, weight_a, len_a), scaled(totals_b, weight_b, len_b)])

    per_pair = lax.map(
        forward_one_pair,
        (
            jnp.moveaxis(
                lax.all_to_all(grid_values, "lat", split_axis=1, concat_axis=2, tiled=True), 1, 0
            ),
            all_tables,
            first_len,
            second_len,
            first_weight,
            second_weight,
        ),
    )
    per_lat = per_pair.transpose(1, 0, 2, 3).reshape(2 * half_dev, 2, wave_count, -1)
    fourier = per_lat.transpose(2, 1, 3, 0)
    picked = fourier[slot_order]
    rates = jnp.repeat(diffusion, LEVELS)
    degree = jnp.arange(wave_count, dtype=jnp.int32)
    ladder = (degree * (degree + 1)).astype(jnp.float32)
    factor = 1.0 / (1.0 + rates[:, None] * (ladder[None, :] / float(wave_count * (wave_count - 1))))
    damping = jnp.where((degree[None, :] >= my_waves[:, None])[:, None, :], factor[None, :, :], 0.0)
    spectral = jnp.einsum(
        "snl,spcl->spcn",
        legendre,
        lax.all_to_all(picked, "lat", split_axis=0, concat_axis=3, tiled=True),
        preferred_element_type=jnp.float32,
    )
    filtered = (spectral * damping[:, None, :, :]).astype(jnp.bfloat16)
    back = jnp.einsum("snl,spcn->spcl", legendre, filtered, preferred_element_type=jnp.float32)
    returned = back.astype(jnp.bfloat16)
    double = jnp.where(wave_ids == 0, 1.0, 2.0).astype(jnp.bfloat16)
    by_wave = lax.all_to_all(returned, "lat", split_axis=3, concat_axis=0, tiled=True)[
        inverse_order
    ]
    real_part = by_wave[:, 0] * double[:, None, None]
    imag_part = -(by_wave[:, 1] * double[:, None, None])
    stacked = jnp.concatenate([real_part, imag_part], axis=0)

    def backward_one_pair(packed):
        coeffs_a, coeffs_b, tables, len_a, len_b = packed
        return inverse_pair(coeffs_a, coeffs_b, tables)

    per_pair = lax.map(
        backward_one_pair,
        (
            jnp.moveaxis(stacked[:, :, :half_dev], 2, 0),
            jnp.moveaxis(stacked[:, :, half_dev:], 2, 0),
            all_tables,
            first_len,
            second_len,
        ),
    )
    rows_out = jnp.moveaxis(per_pair, 0, 1)
    return lax.all_to_all(rows_out, "lat", split_axis=2, concat_axis=1, tiled=True)


SIN_POLY = (3.141592640130707, -5.1677100835078775, 2.550077523214437, -0.5982912856197345, 0.07765766030450941)
COS_POLY = (0.9999999532476085, -4.934792830619644, 4.058411352862619, -1.3318765680811142, 0.2196896110983216)
LANES = 128
SUB = 8
HOPS = (0, 1, 2, 3)
SUM_ORDER = (3, 1, 2, 0)
GATHER_ORDER = (1, 2, 3)
F32 = jnp.float32
BF16 = jnp.bfloat16


def horner(poly, u):
    total = poly[-1]
    for term in poly[-2::-1]:
        total = total * u + term
    return total


def iota(shape, axis):
    return lax.broadcasted_iota(jnp.int32, shape, axis)


def swap_blocks(v):
    sub = iota(v.shape, 1)
    lane = iota(v.shape, 2)
    for bit in range(3):
        step = 1 << bit
        row_bit = (sub >> bit) & 1
        lane_bit = (lane >> (3 + bit)) & 1
        up = pltpu.roll(pltpu.roll(v, SUB - step, 1), SUB * step, 2)
        down = pltpu.roll(pltpu.roll(v, step, 1), LANES - SUB * step, 2)
        v = jnp.where(row_bit == lane_bit, v, jnp.where(row_bit == 0, up, down))
    return v


def pack_kernel(x_ref, o_ref):
    cols, channels, rows = x_ref.shape
    half = channels // 2
    x = x_ref[...].astype(F32)
    v = swap_blocks(jnp.concatenate([x[:, :half], x[:, half:]], axis=2))
    o_ref[...] = v.reshape(cols * SUB, LANES).astype(BF16)


def unpack_kernel(*refs):
    o_ref = refs[-1]
    cols, channels, rows = o_ref.shape
    half = channels // 2
    total = refs[0][...].astype(F32)
    for x_ref in refs[1:-1]:
        total = total + x_ref[...].astype(F32)
    v = swap_blocks(total.reshape(cols, SUB, LANES))
    o_ref[:, :half] = v[:, :, :rows].astype(BF16)
    o_ref[:, half:] = v[:, :, rows:].astype(BF16)


def join_kernel(order, x_ref, y_ref, *o_refs):
    for i, o_ref in zip(order, o_refs):
        o_ref[...] = (x_ref[i].astype(F32) + y_ref[i].astype(F32)).astype(BF16)


def end_kernel(i, x_ref, y_ref, z_ref, o_ref):
    o_ref[...] = (x_ref[i].astype(F32) + y_ref[i].astype(F32) + z_ref[...].astype(F32)).astype(BF16)


def row_lengths(r, half_total):
    quarter = half_total // 2
    lat_total = 2 * half_total
    north = r < quarter
    first = jnp.where(north, r, half_total + r - quarter)
    second = jnp.where(north, half_total - 1 - r, lat_total - 1 - (r - quarter))
    return row_length(first, lat_total), row_length(second, lat_total)


def table_kernel(half_total, cols, waves, device_ref, owner_ref, tt_ref, wave_ref, jf_ref):
    points = tt_ref.shape[1]
    slots = wave_ref.shape[0]
    line = points // (4 * cols)
    device = device_ref[0]
    low = waves // 2
    owned = jnp.where(owner_ref[:, :low] == device, 1.0, 0.0)
    owned = jnp.broadcast_to(owned, (LANES, low)).T
    below = jnp.where(iota((low, low), 1) <= iota((low, low), 0), 1.0, 0.0).astype(BF16)
    count = jnp.dot(below, owned.astype(BF16), preferred_element_type=F32)
    wave_id = iota((low, LANES), 0).astype(F32)
    lane_slot = (iota((low, LANES), 1) % slots).astype(F32)
    hit = (owned > 0.5) & (count - 1.0 == lane_slot)
    wave = jnp.sum(jnp.where(hit, wave_id, 0.0), axis=0, keepdims=True)
    wave_ref[...] = jnp.broadcast_to(wave, (LANES, LANES)).T[:slots]
    place = iota((points, LANES), 0)
    origin = jnp.floor((place.astype(F32) + 0.5) * (1.0 / cols)).astype(jnp.int32)
    rest = place - origin * cols
    part = origin // line
    line_id = origin - part * line
    part = jnp.where(part < 2, 2 * part + 1, 2 * part - 4)
    hop = sum(jnp.where(line_id == i, HOPS[i], 0) for i in range(1, line))
    step = hop * 4 + (part & 1) * 2 + part // 2
    column = (device ^ step) * cols + rest
    jf_ref[...] = column.astype(F32)

    def block(t, carry):
        r = SUB * t + iota((1, LANES), 1) // slots
        len_a, len_b = row_lengths(r, half_total)
        len_a = len_a.astype(F32)
        len_b = len_b.astype(F32)
        inv_a = 1.0 / len_a
        inv_b = 1.0 / len_b
        end_a = jnp.where(2.0 * wave < len_a, len_a, 0.0)
        end_b = jnp.where(2.0 * wave < len_b, len_a + len_b, 0.0)
        for chunk in range(points // 16):
            span = slice(16 * chunk, 16 * chunk + 16)
            jf = jf_ref[span]
            in_a = jf < len_a
            length = jnp.where(in_a, len_a, len_b)
            inverse = jnp.where(in_a, inv_a, inv_b)
            phase = jnp.where(in_a, jf, jf - len_a) * wave
            turns = jnp.floor(phase * inverse + 0.5)
            part = (phase - turns * length) * inverse
            square = part * part
            half_sin = part * horner(SIN_POLY, square)
            half_cos = horner(COS_POLY, square)
            cos_part = 1.0 - 2.0 * (half_sin * half_sin)
            sin_part = 2.0 * (half_sin * half_cos)
            use_a = jf < end_a
            use_b = (jf < end_b) & jnp.logical_not(in_a)
            tt_ref[t, span, 0:LANES] = jnp.where(use_a, cos_part, 0.0).astype(BF16)
            tt_ref[t, span, LANES : 2 * LANES] = jnp.where(use_a, sin_part, 0.0).astype(BF16)
            tt_ref[t, span, 2 * LANES : 3 * LANES] = jnp.where(use_b, cos_part, 0.0).astype(BF16)
            tt_ref[t, span, 3 * LANES : 4 * LANES] = jnp.where(use_b, sin_part, 0.0).astype(BF16)
        return carry

    lax.fori_loop(0, half_total // SUB, block, 0)


def turn_kernel(half_total, tt_ref, weight_ref, rate_ref, tr_ref, scale_ref, factor_ref):
    lat_total = 2 * half_total
    waves = factor_ref.shape[0]

    def block(t, carry):
        for i in range(4):
            lanes = slice(i * LANES, (i + 1) * LANES)
            tr_ref[t, lanes, :] = tt_ref[t, :, lanes].T
        return carry

    lax.fori_loop(0, half_total // SUB, block, 0)
    weight = jnp.broadcast_to(weight_ref[...], (LANES, lat_total)).T
    scale = weight / row_length(iota((lat_total, LANES), 0), lat_total).astype(F32)
    keep = iota((SUB, LANES), 1) % SUB == iota((SUB, LANES), 0)
    quarter = half_total // 2
    for t in range(half_total // SUB):
        r = SUB * t
        if r < quarter:
            first, second = r, half_total - 1 - r
        else:
            first, second = half_total + r - quarter, lat_total - 1 - (r - quarter)
        under = scale[second - SUB + 1 : second + 1]
        under = jnp.concatenate([under[SUB - 1 - i : SUB - i] for i in range(SUB)], axis=0)
        scale_ref[2 * t] = jnp.where(keep, scale[first : first + SUB], 0.0)
        scale_ref[2 * t + 1] = jnp.where(keep, under, 0.0)
    fields = rate_ref.shape[1]
    field = iota((1, LANES), 1) % (LANES // SUB) // LEVELS
    rate = jnp.zeros((1, LANES), F32)
    for i in range(fields):
        rate = jnp.where(field == i, rate_ref[:, i : i + 1], rate)
    degree = iota((waves, LANES), 0)
    ladder = (degree * (degree + 1)).astype(F32) / float(waves * (waves - 1))
    factor_ref[...] = 1.0 / (1.0 + rate * ladder)


def main_kernel(
    x0_ref, x1_ref, x2_ref, x3_ref, tt_ref, tr_ref, wave_ref, scale_ref, factor_ref, leg_ref, o1_ref, o3_ref, rhs_ref, z_ref, at_ref, bt_ref
):
    blocks, points, _ = tt_ref.shape
    slots, waves, lat_total = leg_ref.shape
    line, lines, _ = x0_ref.shape
    for i, x_ref in enumerate((x1_ref, x3_ref, x0_ref, x2_ref)):
        for j in range(line):
            z_ref[(i * line + j) * lines : (i * line + j + 1) * lines] = x_ref[j].astype(F32)
    row2 = iota((2 * LANES, LANES), 0)
    col2 = iota((2 * LANES, LANES), 1)
    gather = jnp.where(row2 // SUB == col2, jnp.where(row2 < LANES, 1.0, -1.0), 0.0).astype(BF16)
    row3 = iota((LANES, 2 * LANES), 0)
    col3 = iota((LANES, 2 * LANES), 1)
    spread = jnp.where(col3 // SUB == row3, jnp.where(col3 < LANES, 1.0, -1.0), 0.0).astype(BF16)
    slab = SUB * slots // 2

    def forward(t, carry):
        z = z_ref[pl.ds(t, points, stride=SUB), :].astype(BF16)
        d = jnp.dot(tr_ref[t], z, preferred_element_type=F32)
        for h in range(2):
            parts = []
            for p in range(2):
                base = (2 * h + p) * LANES
                rows = [
                    d[base + i * slots : base + (i + 1) * slots] * scale_ref[2 * t + h, i : i + 1, :]
                    for i in range(SUB)
                ]
                parts.append(jnp.concatenate(rows, axis=0).astype(BF16))
            a = jnp.dot(jnp.concatenate(parts, axis=1), gather, preferred_element_type=F32)
            for i in range(2):
                at_ref[pl.ds(pl.multiple_of((2 * t + i) * LANES + h * slab, SUB), slab), :] = a[i * slab : (i + 1) * slab]
        return carry

    lax.fori_loop(0, blocks, forward, 0, unroll=8)
    degree = iota((waves, LANES), 0).astype(F32)

    def slot(s, carry):
        f = at_ref[pl.ds(s, lat_total, stride=slots), :].astype(BF16)
        table = leg_ref[s]
        spectral = jnp.dot(table, f, preferred_element_type=F32)
        wave = wave_ref[pl.ds(s, 1), :]
        kept = jnp.where(degree >= wave, spectral * factor_ref[...], 0.0).astype(BF16)
        back = lax.dot_general(table, kept, (((0,), (0,)), ((), ())), preferred_element_type=F32)
        back = back.astype(BF16).astype(F32) * jnp.where(wave == 0.0, 1.0, 2.0)
        bt_ref[pl.ds(s, lat_total, stride=slots), :] = back
        return carry

    lax.fori_loop(0, slots, slot, 0, unroll=16)
    reach = -(points // 2) // 16 * -16
    keep = (iota((LANES, 2 * LANES), 1) % SUB) == iota((LANES, 2 * LANES), 0) // slots

    def inverse(t, carry):
        rhs = []
        for h in range(2):
            b = jnp.concatenate(
                [bt_ref[pl.ds(pl.multiple_of((2 * t + i) * LANES + h * slab, SUB), slab), :] for i in range(2)], axis=0
            ).astype(BF16)
            wide = jnp.dot(b, spread, preferred_element_type=F32)
            wide = jnp.where(keep, wide, 0.0).astype(BF16)
            rhs.append(wide[:, :LANES])
            rhs.append(wide[:, LANES:])
        rhs = jnp.concatenate(rhs, axis=0)
        rhs_ref[t] = rhs
        out = jnp.dot(tt_ref[t, :reach], rhs, preferred_element_type=F32)
        z_ref[pl.ds(t, points // 2, stride=SUB), :] = out[: points // 2]
        return carry

    lax.fori_loop(0, blocks, inverse, 0, unroll=8)
    for i, o_ref in enumerate((o1_ref, o3_ref)):
        for j in range(line):
            o_ref[j] = z_ref[(i * line + j) * lines : (i * line + j + 1) * lines].astype(BF16)


def near_kernel(tt_ref, rhs_ref, o0_ref, o2_ref, z_ref):
    blocks, points, _ = tt_ref.shape
    line, lines, _ = o0_ref.shape
    from_row = points // 2 // 16 * 16

    def inverse(t, carry):
        out = jnp.dot(tt_ref[t, from_row:], rhs_ref[t], preferred_element_type=F32)
        z_ref[pl.ds(t, points // 2, stride=SUB), :] = out[points // 2 - from_row :]
        return carry

    lax.fori_loop(0, blocks, inverse, 0, unroll=8)
    for i, o_ref in enumerate((o0_ref, o2_ref)):
        for j in range(line):
            o_ref[j] = z_ref[(i * line + j) * lines : (i * line + j + 1) * lines].astype(BF16)


def kernel_call(body, out_shape, in_specs, scratch=(), flops=0, moved=0):
    return pl.pallas_call(
        body,
        out_shape=out_shape,
        in_specs=in_specs,
        scratch_shapes=list(scratch),
        compiler_params=pltpu.CompilerParams(vmem_limit_bytes=12 << 20),
        cost_estimate=pl.CostEstimate(flops=flops, bytes_accessed=moved, transcendentals=0),
    )


def transform_call(parts, tt, tr, wave, scale, factor, legendre):
    slots = wave.shape[0]
    waves, lat_total = legendre.shape[1:]
    line, lines, _ = parts[0].shape
    whole = pl.BlockSpec(memory_space=pltpu.VMEM)
    return pl.pallas_call(
        main_kernel,
        out_shape=[jax.ShapeDtypeStruct((line, lines, LANES), BF16)] * 2
        + [jax.ShapeDtypeStruct(tt.shape[:1] + (4 * LANES, LANES), BF16)],
        in_specs=[whole] * 10,
        out_specs=[whole] * 3,
        scratch_shapes=[
            pltpu.VMEM((4 * line * lines, LANES), F32),
            pltpu.VMEM((lat_total * slots, LANES), F32),
            pltpu.VMEM((lat_total * slots, LANES), F32),
        ],
        compiler_params=pltpu.CompilerParams(vmem_limit_bytes=16 << 20),
    )(*parts, tt, tr, wave, scale, factor, legendre)


def short_rows_body(grid_values, quad_weights, owner_map, legendre, diffusion):
    channels, half_total, cols = grid_values.shape
    groups = lax.axis_size("lat")
    line = groups // 4
    device = lax.axis_index("lat").astype(jnp.int32)
    waves = legendre.shape[1]
    lat_total = legendre.shape[2]
    slots = legendre.shape[0] // 2
    blocks = half_total // SUB
    points = cols * groups
    lines = cols * SUB
    whole = pl.BlockSpec(memory_space=pltpu.VMEM)
    shape = jax.ShapeDtypeStruct
    with jax.named_scope("pack"):
        mine = kernel_call(pack_kernel, shape((lines, LANES), BF16), [whole])(jnp.transpose(grid_values, (2, 0, 1)))

    def across(x, step):
        return lax.ppermute(x, "lat", [(i, i ^ step) for i in range(groups)])

    with jax.named_scope("gather_line"):
        arrived = {hop: across(mine, 4 * hop) for hop in GATHER_ORDER}
        arrived = [arrived[hop] for hop in HOPS[1:]]
    with jax.named_scope("tables"):
        tt, wave = kernel_call(
            functools.partial(table_kernel, half_total, cols, waves),
            (shape((blocks, points, 4 * LANES), BF16), shape((slots, LANES), F32)),
            [pl.BlockSpec(memory_space=pltpu.SMEM), whole],
            [pltpu.VMEM((points, LANES), F32)],
            flops=12 << 20,
            moved=3 << 20,
        )(device[None], owner_map[None, :])
        arrived, tt, wave = lax.optimization_barrier((arrived, tt, wave))
    with jax.named_scope("gather_line"):
        p0 = jnp.stack([mine] + arrived)
    with jax.named_scope("gather_plane"):
        p1 = across(p0, 2)
        tr, scale, factor = kernel_call(
            functools.partial(turn_kernel, half_total),
            (
                shape((blocks, 4 * LANES, points), BF16),
                shape((2 * blocks, SUB, LANES), F32),
                shape((waves, LANES), F32),
            ),
            [whole, whole, whole],
            flops=12 << 20,
            moved=6 << 20,
        )(tt, quad_weights[None, :], diffusion[None, :])
        half_legendre = legendre[:slots]
        p1, tr, scale, factor, half_legendre = lax.optimization_barrier((p1, tr, scale, factor, half_legendre))
        p2 = across(p0, 1)
        p3 = across(p1, 1)
    with jax.named_scope("transform"):
        s1, s3, rhs = transform_call((p0, p1, p2, p3), tt, tr, wave, scale, factor, half_legendre)
    block = shape((line, lines, LANES), BF16)
    with jax.named_scope("sum_cores"):
        r3 = across(s3, 1)
        s0, s2 = kernel_call(near_kernel, [block] * 2, [whole] * 2, [pltpu.VMEM((2 * line * lines, LANES), F32)])(tt, rhs)
        one = shape((lines, LANES), BF16)
        sums = kernel_call(functools.partial(join_kernel, SUM_ORDER), [one] * line, [whole] * 2)(s1, r3)
        r2 = across(s2, 1)
    with jax.named_scope("sum_plane"):
        sums = [across(piece, 2) for piece in sums]
    with jax.named_scope("sum_line"):
        ready = []
        for i, piece in zip(SUM_ORDER, sums):
            end = kernel_call(functools.partial(end_kernel, i), one, [whole] * 3)(s0, r2, piece)
            ready.append(across(end, 4 * HOPS[i]) if i else end)
    with jax.named_scope("unpack"):
        out = kernel_call(unpack_kernel, shape((cols, channels, half_total), BF16), [whole] * line)(*ready)
    return jnp.transpose(out, (1, 2, 0))


def body(grid_values, quad_weights, owner_map, legendre, diffusion):
    channels, half_total, cols = grid_values.shape
    slots, waves, lat_total = legendre.shape
    groups = lax.axis_size("lat")
    longest = 20 + 4 * (half_total - 1)
    short = (
        longest <= waves
        and groups >= 8
        and groups & (groups - 1) == 0
        and half_total % groups == 0
        and half_total // groups * 2 == SUB
        and groups == 4 * len(HOPS)
        and channels * SUB == LANES
        and channels * half_total == SUB * LANES
        and slots * SUB == 2 * LANES
        and lat_total == LANES
        and cols * groups % 16 == 0
    )
    if short:
        return short_rows_body(grid_values, quad_weights, owner_map, legendre, diffusion)
    return any_rows_body(grid_values, quad_weights, owner_map, legendre, diffusion)


def solution(mesh):
    return jax.shard_map(
        body,
        mesh=mesh,
        in_specs=(P("grp", None, "lat"), P(), P(), P("lat", None, None), P()),
        out_specs=P("grp", None, "lat"),
        check_vma=False,
    )
```

```python
import functools
import math

import jax
import jax.numpy as jnp
from jax import lax
from jax.experimental import pallas as pl
from jax.experimental.pallas import tpu as pltpu
from jax.sharding import PartitionSpec as P

LEVELS = 4


TWO_PI = 2.0 * math.pi


def pair_rows(lat_total):
    half = lat_total // 2
    quarter = lat_total // 4
    pair_ids = jnp.arange(half, dtype=jnp.int32)
    north = pair_ids < quarter
    shifted = pair_ids - quarter
    first = jnp.where(north, pair_ids, half + shifted)
    second = jnp.where(north, half - 1 - pair_ids, lat_total - 1 - shifted)
    return (first, second)


def row_length(lat_ids, lat_total):
    return 20 + 4 * jnp.minimum(lat_ids, lat_total - 1 - lat_ids)


def trig_table(length, offset, col_count, wave_ids):
    col_ids = jnp.arange(col_count, dtype=jnp.int32)
    local = col_ids - offset
    phases = local[:, None] * wave_ids[None, :] % length
    angles = phases.astype(jnp.float32) / length.astype(jnp.float32) * TWO_PI
    usable = (local[:, None] >= 0) & (local[:, None] < length) & (2 * wave_ids[None, :] < length)
    cos_part = jnp.where(usable, jnp.cos(angles), 0.0).astype(jnp.bfloat16)
    sin_part = jnp.where(usable, jnp.sin(angles), 0.0).astype(jnp.bfloat16)
    return jnp.concatenate([cos_part, sin_part], axis=1)


def any_rows_body(grid_values, quad_weights, owner_map, legendre, diffusion):
    channels, half_total, col_dev = grid_values.shape
    groups = lax.axis_size("lat")
    device = lax.axis_index("lat")
    half_dev = half_total // groups
    lat_total = 2 * half_total
    row_width = col_dev * groups
    owned_slots = legendre.shape[0]
    wave_count = legendre.shape[1]
    wave_ids = jnp.arange(wave_count, dtype=jnp.int32)
    slot_order = jnp.argsort(owner_map, stable=True)
    inverse_order = jnp.argsort(slot_order)
    my_waves = lax.dynamic_slice_in_dim(slot_order, device * owned_slots, owned_slots)
    contract = (((0,), (1,)), ((), ()))
    first, second = pair_rows(lat_total)
    my_first = lax.dynamic_slice_in_dim(first, device * half_dev, half_dev)
    my_second = lax.dynamic_slice_in_dim(second, device * half_dev, half_dev)
    first_len = row_length(my_first, lat_total)
    second_len = row_length(my_second, lat_total)
    first_weight = jnp.take(quad_weights, my_first)
    second_weight = jnp.take(quad_weights, my_second)

    def pair_tables(packed):
        len_a, len_b = packed
        return jnp.concatenate(
            [
                trig_table(len_a, 0, row_width, wave_ids),
                trig_table(len_b, len_a, row_width, wave_ids),
            ],
            axis=1,
        )

    all_tables = lax.map(pair_tables, (first_len, second_len))

    def forward_pair(row_data, tables):
        totals = lax.dot_general(tables, row_data, contract, preferred_element_type=jnp.float32)
        return (totals[: 2 * wave_count], totals[2 * wave_count :])

    def inverse_pair(coeffs_a, coeffs_b, tables):
        joined = jnp.concatenate([coeffs_a, coeffs_b], axis=0)
        return lax.dot_general(joined, tables, contract, preferred_element_type=jnp.float32).astype(
            jnp.bfloat16
        )

    def scaled(totals, weight, length):
        row_scale = weight / length.astype(jnp.float32)
        return jnp.concatenate(
            [totals[:wave_count] * row_scale, totals[wave_count:] * -row_scale], axis=0
        ).astype(jnp.bfloat16)

    def forward_one_pair(packed):
        row_data, tables, len_a, len_b, weight_a, weight_b = packed
        totals_a, totals_b = forward_pair(row_data, tables)
        return jnp.stack([scaled(totals_a, weight_a, len_a), scaled(totals_b, weight_b, len_b)])

    per_pair = lax.map(
        forward_one_pair,
        (
            jnp.moveaxis(
                lax.all_to_all(grid_values, "lat", split_axis=1, concat_axis=2, tiled=True), 1, 0
            ),
            all_tables,
            first_len,
            second_len,
            first_weight,
            second_weight,
        ),
    )
    per_lat = per_pair.transpose(1, 0, 2, 3).reshape(2 * half_dev, 2, wave_count, -1)
    fourier = per_lat.transpose(2, 1, 3, 0)
    picked = fourier[slot_order]
    rates = jnp.repeat(diffusion, LEVELS)
    degree = jnp.arange(wave_count, dtype=jnp.int32)
    ladder = (degree * (degree + 1)).astype(jnp.float32)
    factor = 1.0 / (1.0 + rates[:, None] * (ladder[None, :] / float(wave_count * (wave_count - 1))))
    damping = jnp.where((degree[None, :] >= my_waves[:, None])[:, None, :], factor[None, :, :], 0.0)
    spectral = jnp.einsum(
        "snl,spcl->spcn",
        legendre,
        lax.all_to_all(picked, "lat", split_axis=0, concat_axis=3, tiled=True),
        preferred_element_type=jnp.float32,
    )
    filtered = (spectral * damping[:, None, :, :]).astype(jnp.bfloat16)
    back = jnp.einsum("snl,spcn->spcl", legendre, filtered, preferred_element_type=jnp.float32)
    returned = back.astype(jnp.bfloat16)
    double = jnp.where(wave_ids == 0, 1.0, 2.0).astype(jnp.bfloat16)
    by_wave = lax.all_to_all(returned, "lat", split_axis=3, concat_axis=0, tiled=True)[
        inverse_order
    ]
    real_part = by_wave[:, 0] * double[:, None, None]
    imag_part = -(by_wave[:, 1] * double[:, None, None])
    stacked = jnp.concatenate([real_part, imag_part], axis=0)

    def backward_one_pair(packed):
        coeffs_a, coeffs_b, tables, len_a, len_b = packed
        return inverse_pair(coeffs_a, coeffs_b, tables)

    per_pair = lax.map(
        backward_one_pair,
        (
            jnp.moveaxis(stacked[:, :, :half_dev], 2, 0),
            jnp.moveaxis(stacked[:, :, half_dev:], 2, 0),
            all_tables,
            first_len,
            second_len,
        ),
    )
    rows_out = jnp.moveaxis(per_pair, 0, 1)
    return lax.all_to_all(rows_out, "lat", split_axis=2, concat_axis=1, tiled=True)


SIN_POLY = (4.44288291912434, -7.30824568650904, 3.60635421843265, -0.846111650373064, 0.1098245164248)
COS_POLY = (1.41421349625523, -6.97885094856382, 5.73946037690726, -1.88355790598724, 0.310688027527717)
LANES = 128
SUB = 8
HOPS = (0, 1, 2, 3)
SUM_ORDER = (3, 1, 2, 0)
GATHER_ORDER = (1, 2, 3)
F32 = jnp.float32
BF16 = jnp.bfloat16


def horner(poly, u):
    total = poly[-1]
    for term in poly[-2::-1]:
        total = total * u + term
    return total


def iota(shape, axis):
    return lax.broadcasted_iota(jnp.int32, shape, axis)


def swap_blocks(v):
    sub = iota(v.shape, 1)
    lane = iota(v.shape, 2)
    for bit in range(3):
        step = 1 << bit
        row_bit = (sub >> bit) & 1
        lane_bit = (lane >> (3 + bit)) & 1
        up = pltpu.roll(pltpu.roll(v, SUB - step, 1), SUB * step, 2)
        down = pltpu.roll(pltpu.roll(v, step, 1), LANES - SUB * step, 2)
        v = jnp.where(row_bit == lane_bit, v, jnp.where(row_bit == 0, up, down))
    return v


def pack_kernel(x_ref, o_ref):
    cols, channels, rows = x_ref.shape
    half = channels // 2
    x = x_ref[...].astype(F32)
    v = swap_blocks(jnp.concatenate([x[:, :half], x[:, half:]], axis=2))
    o_ref[...] = v.reshape(cols * SUB, LANES).astype(BF16)


def unpack_kernel(*refs):
    o_ref = refs[-1]
    cols, channels, rows = o_ref.shape
    half = channels // 2
    total = refs[0][...].astype(F32)
    for x_ref in refs[1:-1]:
        total = total + x_ref[...].astype(F32)
    v = swap_blocks(total.reshape(cols, SUB, LANES))
    o_ref[:, :half] = v[:, :, :rows].astype(BF16)
    o_ref[:, half:] = v[:, :, rows:].astype(BF16)


def join_kernel(order, x_ref, y_ref, *o_refs):
    for i, o_ref in zip(order, o_refs):
        o_ref[...] = (x_ref[i].astype(F32) + y_ref[i].astype(F32)).astype(BF16)


def end_kernel(i, x_ref, y_ref, z_ref, o_ref):
    o_ref[...] = (x_ref[i].astype(F32) + y_ref[i].astype(F32) + z_ref[...].astype(F32)).astype(BF16)


def row_lengths(r, half_total):
    quarter = half_total // 2
    lat_total = 2 * half_total
    north = r < quarter
    first = jnp.where(north, r, half_total + r - quarter)
    second = jnp.where(north, half_total - 1 - r, lat_total - 1 - (r - quarter))
    return row_length(first, lat_total), row_length(second, lat_total)


def table_kernel(half_total, cols, waves, device_ref, owner_ref, tt_ref, wave_ref, jf_ref):
    points = tt_ref.shape[1]
    slots = wave_ref.shape[0]
    line = points // (4 * cols)
    device = device_ref[0]
    low = waves // 2
    owned = jnp.where(owner_ref[:, :low] == device, 1.0, 0.0)
    owned = jnp.broadcast_to(owned, (LANES, low)).T
    below = jnp.where(iota((low, low), 1) <= iota((low, low), 0), 1.0, 0.0).astype(BF16)
    count = jnp.dot(below, owned.astype(BF16), preferred_element_type=F32)
    wave_id = iota((low, LANES), 0).astype(F32)
    lane_slot = (iota((low, LANES), 1) % slots).astype(F32)
    hit = (owned > 0.5) & (count - 1.0 == lane_slot)
    wave = jnp.sum(jnp.where(hit, wave_id, 0.0), axis=0, keepdims=True)
    wave_ref[...] = jnp.broadcast_to(wave, (LANES, LANES)).T[:slots]
    place = iota((points, LANES), 0)
    origin = jnp.floor((place.astype(F32) + 0.5) * (1.0 / cols)).astype(jnp.int32)
    rest = place - origin * cols
    part = origin // line
    line_id = origin - part * line
    part = jnp.where(part < 2, 2 * part + 1, 2 * part - 4)
    hop = sum(jnp.where(line_id == i, HOPS[i], 0) for i in range(1, line))
    step = hop * 4 + (part & 1) * 2 + part // 2
    column = (device ^ step) * cols + rest
    jf_ref[...] = column.astype(F32)

    def block(t, carry):
        r = SUB * t + iota((1, LANES), 1) // slots
        len_a, len_b = row_lengths(r, half_total)
        len_a = len_a.astype(F32)
        len_b = len_b.astype(F32)
        rate_a = wave / len_a
        rate_b = wave / len_b
        end_a = jnp.where(2.0 * wave < len_a, len_a, 0.0)
        end_b = jnp.where(2.0 * wave < len_b, len_a + len_b, 0.0)
        for chunk in range(points // 16):
            span = slice(16 * chunk, 16 * chunk + 16)
            jf = jf_ref[span]
            in_a = jf < len_a
            turns = jnp.where(in_a, jf, jf - len_a) * jnp.where(in_a, rate_a, rate_b)
            part = turns - jnp.round(turns)
            square = part * part
            half_sin = part * horner(SIN_POLY, square)
            half_cos = horner(COS_POLY, square)
            cos_part = 1.0 - half_sin * half_sin
            sin_part = half_sin * half_cos
            use_a = jf < end_a
            use_b = (jf < end_b) & jnp.logical_not(in_a)
            tt_ref[t, span, 0:LANES] = jnp.where(use_a, cos_part, 0.0).astype(BF16)
            tt_ref[t, span, LANES : 2 * LANES] = jnp.where(use_a, sin_part, 0.0).astype(BF16)
            tt_ref[t, span, 2 * LANES : 3 * LANES] = jnp.where(use_b, cos_part, 0.0).astype(BF16)
            tt_ref[t, span, 3 * LANES : 4 * LANES] = jnp.where(use_b, sin_part, 0.0).astype(BF16)
        return carry

    lax.fori_loop(0, half_total // SUB, block, 0)


def turn_kernel(half_total, tt_ref, weight_ref, rate_ref, tr_ref, scale_ref, factor_ref):
    lat_total = 2 * half_total
    waves = factor_ref.shape[0]

    def block(t, carry):
        for i in range(4):
            lanes = slice(i * LANES, (i + 1) * LANES)
            tr_ref[t, lanes, :] = tt_ref[t, :, lanes].T
        return carry

    lax.fori_loop(0, half_total // SUB, block, 0)
    weight = jnp.broadcast_to(weight_ref[...], (LANES, lat_total)).T
    scale = weight / row_length(iota((lat_total, LANES), 0), lat_total).astype(F32)
    keep = iota((SUB, LANES), 1) % SUB == iota((SUB, LANES), 0)
    quarter = half_total // 2
    for t in range(half_total // SUB):
        r = SUB * t
        if r < quarter:
            first, second = r, half_total - 1 - r
        else:
            first, second = half_total + r - quarter, lat_total - 1 - (r - quarter)
        under = scale[second - SUB + 1 : second + 1]
        under = jnp.concatenate([under[SUB - 1 - i : SUB - i] for i in range(SUB)], axis=0)
        scale_ref[2 * t] = jnp.where(keep, scale[first : first + SUB], 0.0)
        scale_ref[2 * t + 1] = jnp.where(keep, under, 0.0)
    fields = rate_ref.shape[1]
    field = iota((1, LANES), 1) % (LANES // SUB) // LEVELS
    rate = jnp.zeros((1, LANES), F32)
    for i in range(fields):
        rate = jnp.where(field == i, rate_ref[:, i : i + 1], rate)
    degree = iota((waves, LANES), 0)
    ladder = (degree * (degree + 1)).astype(F32) / float(waves * (waves - 1))
    factor_ref[...] = 1.0 / (1.0 + rate * ladder)


def main_kernel(
    x0_ref, x1_ref, x2_ref, x3_ref, tt_ref, tr_ref, wave_ref, scale_ref, factor_ref, leg_ref, o1_ref, o3_ref, rhs_ref, z_ref, at_ref, bt_ref
):
    blocks, points, _ = tt_ref.shape
    slots, waves, lat_total = leg_ref.shape
    line, lines, _ = x0_ref.shape
    for i, x_ref in enumerate((x1_ref, x3_ref, x0_ref, x2_ref)):
        for j in range(line):
            z_ref[(i * line + j) * lines : (i * line + j + 1) * lines] = x_ref[j].astype(F32)
    row2 = iota((2 * LANES, LANES), 0)
    col2 = iota((2 * LANES, LANES), 1)
    gather = jnp.where(row2 // SUB == col2, jnp.where(row2 < LANES, 1.0, -1.0), 0.0).astype(BF16)
    row3 = iota((LANES, 2 * LANES), 0)
    col3 = iota((LANES, 2 * LANES), 1)
    spread = jnp.where(col3 // SUB == row3, jnp.where(col3 < LANES, 1.0, -1.0), 0.0).astype(BF16)
    slab = SUB * slots // 2

    def forward(t, carry):
        z = z_ref[pl.ds(t, points, stride=SUB), :].astype(BF16)
        d = jnp.dot(tr_ref[t], z, preferred_element_type=F32)
        for h in range(2):
            parts = []
            for p in range(2):
                base = (2 * h + p) * LANES
                rows = [
                    d[base + i * slots : base + (i + 1) * slots] * scale_ref[2 * t + h, i : i + 1, :]
                    for i in range(SUB)
                ]
                parts.append(jnp.concatenate(rows, axis=0).astype(BF16))
            a = jnp.dot(jnp.concatenate(parts, axis=1), gather, preferred_element_type=F32)
            for i in range(2):
                at_ref[pl.ds(pl.multiple_of((2 * t + i) * LANES + h * slab, SUB), slab), :] = a[i * slab : (i + 1) * slab]
        return carry

    lax.fori_loop(0, blocks, forward, 0, unroll=8)
    degree = iota((waves, LANES), 0).astype(F32)

    def slot(s, carry):
        f = at_ref[pl.ds(s, lat_total, stride=slots), :].astype(BF16)
        table = leg_ref[s]
        spectral = jnp.dot(table, f, preferred_element_type=F32)
        wave = wave_ref[pl.ds(s, 1), :]
        kept = jnp.where(degree >= wave, spectral * factor_ref[...], 0.0).astype(BF16)
        back = lax.dot_general(table, kept, (((0,), (0,)), ((), ())), preferred_element_type=F32)
        back = back.astype(BF16).astype(F32) * jnp.where(wave == 0.0, 1.0, 2.0)
        bt_ref[pl.ds(s, lat_total, stride=slots), :] = back
        return carry

    lax.fori_loop(0, slots, slot, 0, unroll=16)
    reach = -(points // 2) // 16 * -16
    keep = (iota((LANES, 2 * LANES), 1) % SUB) == iota((LANES, 2 * LANES), 0) // slots

    def inverse(t, carry):
        rhs = []
        for h in range(2):
            b = jnp.concatenate(
                [bt_ref[pl.ds(pl.multiple_of((2 * t + i) * LANES + h * slab, SUB), slab), :] for i in range(2)], axis=0
            ).astype(BF16)
            wide = jnp.dot(b, spread, preferred_element_type=F32)
            wide = jnp.where(keep, wide, 0.0).astype(BF16)
            rhs.append(wide[:, :LANES])
            rhs.append(wide[:, LANES:])
        rhs = jnp.concatenate(rhs, axis=0)
        rhs_ref[t] = rhs
        out = jnp.dot(tt_ref[t, :reach], rhs, preferred_element_type=F32)
        z_ref[pl.ds(t, points // 2, stride=SUB), :] = out[: points // 2]
        return carry

    lax.fori_loop(0, blocks, inverse, 0, unroll=8)
    for i, o_ref in enumerate((o1_ref, o3_ref)):
        for j in range(line):
            o_ref[j] = z_ref[(i * line + j) * lines : (i * line + j + 1) * lines].astype(BF16)


def near_kernel(tt_ref, rhs_ref, o0_ref, o2_ref, z_ref):
    blocks, points, _ = tt_ref.shape
    line, lines, _ = o0_ref.shape
    from_row = points // 2 // 16 * 16

    def inverse(t, carry):
        out = jnp.dot(tt_ref[t, from_row:], rhs_ref[t], preferred_element_type=F32)
        z_ref[pl.ds(t, points // 2, stride=SUB), :] = out[points // 2 - from_row :]
        return carry

    lax.fori_loop(0, blocks, inverse, 0, unroll=8)
    for i, o_ref in enumerate((o0_ref, o2_ref)):
        for j in range(line):
            o_ref[j] = z_ref[(i * line + j) * lines : (i * line + j + 1) * lines].astype(BF16)


def kernel_call(body, out_shape, in_specs, scratch=(), flops=0, moved=0):
    return pl.pallas_call(
        body,
        out_shape=out_shape,
        in_specs=in_specs,
        scratch_shapes=list(scratch),
        compiler_params=pltpu.CompilerParams(vmem_limit_bytes=12 << 20),
        cost_estimate=pl.CostEstimate(flops=flops, bytes_accessed=moved, transcendentals=0),
    )


def transform_call(parts, tt, tr, wave, scale, factor, legendre):
    slots = wave.shape[0]
    waves, lat_total = legendre.shape[1:]
    line, lines, _ = parts[0].shape
    whole = pl.BlockSpec(memory_space=pltpu.VMEM)
    return pl.pallas_call(
        main_kernel,
        out_shape=[jax.ShapeDtypeStruct((line, lines, LANES), BF16)] * 2
        + [jax.ShapeDtypeStruct(tt.shape[:1] + (4 * LANES, LANES), BF16)],
        in_specs=[whole] * 10,
        out_specs=[whole] * 3,
        scratch_shapes=[
            pltpu.VMEM((4 * line * lines, LANES), F32),
            pltpu.VMEM((lat_total * slots, LANES), F32),
            pltpu.VMEM((lat_total * slots, LANES), F32),
        ],
        compiler_params=pltpu.CompilerParams(vmem_limit_bytes=16 << 20),
    )(*parts, tt, tr, wave, scale, factor, legendre)


def short_rows_body(grid_values, quad_weights, owner_map, legendre, diffusion):
    channels, half_total, cols = grid_values.shape
    groups = lax.axis_size("lat")
    line = groups // 4
    device = lax.axis_index("lat").astype(jnp.int32)
    waves = legendre.shape[1]
    lat_total = legendre.shape[2]
    slots = legendre.shape[0] // 2
    blocks = half_total // SUB
    points = cols * groups
    lines = cols * SUB
    whole = pl.BlockSpec(memory_space=pltpu.VMEM)
    shape = jax.ShapeDtypeStruct
    with jax.named_scope("pack"):
        mine = kernel_call(pack_kernel, shape((lines, LANES), BF16), [whole])(jnp.transpose(grid_values, (2, 0, 1)))

    def across(x, step):
        return lax.ppermute(x, "lat", [(i, i ^ step) for i in range(groups)])

    with jax.named_scope("gather_line"):
        arrived = {hop: across(mine, 4 * hop) for hop in GATHER_ORDER}
        arrived = [arrived[hop] for hop in HOPS[1:]]
    with jax.named_scope("tables"):
        tt, wave = kernel_call(
            functools.partial(table_kernel, half_total, cols, waves),
            (shape((blocks, points, 4 * LANES), BF16), shape((slots, LANES), F32)),
            [pl.BlockSpec(memory_space=pltpu.SMEM), whole],
            [pltpu.VMEM((points, LANES), F32)],
            flops=12 << 20,
            moved=3 << 20,
        )(device[None], owner_map[None, :])
        arrived, tt, wave = lax.optimization_barrier((arrived, tt, wave))
    with jax.named_scope("gather_line"):
        p0 = jnp.stack([mine] + arrived)
    with jax.named_scope("gather_plane"):
        p1 = across(p0, 2)
        tr, scale, factor = kernel_call(
            functools.partial(turn_kernel, half_total),
            (
                shape((blocks, 4 * LANES, points), BF16),
                shape((2 * blocks, SUB, LANES), F32),
                shape((waves, LANES), F32),
            ),
            [whole, whole, whole],
            flops=12 << 20,
            moved=6 << 20,
        )(tt, quad_weights[None, :], diffusion[None, :])
        half_legendre = legendre[:slots]
        p1, tr, scale, factor, half_legendre = lax.optimization_barrier((p1, tr, scale, factor, half_legendre))
        p2 = across(p0, 1)
        p3 = across(p1, 1)
    with jax.named_scope("transform"):
        s1, s3, rhs = transform_call((p0, p1, p2, p3), tt, tr, wave, scale, factor, half_legendre)
    block = shape((line, lines, LANES), BF16)
    with jax.named_scope("sum_cores"):
        r3 = across(s3, 1)
        s0, s2 = kernel_call(near_kernel, [block] * 2, [whole] * 2, [pltpu.VMEM((2 * line * lines, LANES), F32)])(tt, rhs)
        one = shape((lines, LANES), BF16)
        sums = kernel_call(functools.partial(join_kernel, SUM_ORDER), [one] * line, [whole] * 2)(s1, r3)
        r2 = across(s2, 1)
    with jax.named_scope("sum_plane"):
        sums = [across(piece, 2) for piece in sums]
    with jax.named_scope("sum_line"):
        ready = []
        for i, piece in zip(SUM_ORDER, sums):
            end = kernel_call(functools.partial(end_kernel, i), one, [whole] * 3)(s0, r2, piece)
            ready.append(across(end, 4 * HOPS[i]) if i else end)
    with jax.named_scope("unpack"):
        out = kernel_call(unpack_kernel, shape((cols, channels, half_total), BF16), [whole] * line)(*ready)
    return jnp.transpose(out, (1, 2, 0))


def body(grid_values, quad_weights, owner_map, legendre, diffusion):
    channels, half_total, cols = grid_values.shape
    slots, waves, lat_total = legendre.shape
    groups = lax.axis_size("lat")
    longest = 20 + 4 * (half_total - 1)
    short = (
        longest <= waves
        and groups >= 8
        and groups & (groups - 1) == 0
        and half_total % groups == 0
        and half_total // groups * 2 == SUB
        and groups == 4 * len(HOPS)
        and channels * SUB == LANES
        and channels * half_total == SUB * LANES
        and slots * SUB == 2 * LANES
        and lat_total == LANES
        and cols * groups % 16 == 0
    )
    if short:
        return short_rows_body(grid_values, quad_weights, owner_map, legendre, diffusion)
    return any_rows_body(grid_values, quad_weights, owner_map, legendre, diffusion)


def solution(mesh):
    return jax.shard_map(
        body,
        mesh=mesh,
        in_specs=(P("grp", None, "lat"), P(), P(), P("lat", None, None), P()),
        out_specs=P("grp", None, "lat"),
        check_vma=False,
    )
```

```python
import functools
import math

import jax
import jax.numpy as jnp
from jax import lax
from jax.experimental import pallas as pl
from jax.experimental.pallas import tpu as pltpu
from jax.sharding import PartitionSpec as P

LEVELS = 4


TWO_PI = 2.0 * math.pi


def pair_rows(lat_total):
    half = lat_total // 2
    quarter = lat_total // 4
    pair_ids = jnp.arange(half, dtype=jnp.int32)
    north = pair_ids < quarter
    shifted = pair_ids - quarter
    first = jnp.where(north, pair_ids, half + shifted)
    second = jnp.where(north, half - 1 - pair_ids, lat_total - 1 - shifted)
    return (first, second)


def row_length(lat_ids, lat_total):
    return 20 + 4 * jnp.minimum(lat_ids, lat_total - 1 - lat_ids)


def trig_table(length, offset, col_count, wave_ids):
    col_ids = jnp.arange(col_count, dtype=jnp.int32)
    local = col_ids - offset
    phases = local[:, None] * wave_ids[None, :] % length
    angles = phases.astype(jnp.float32) / length.astype(jnp.float32) * TWO_PI
    usable = (local[:, None] >= 0) & (local[:, None] < length) & (2 * wave_ids[None, :] < length)
    cos_part = jnp.where(usable, jnp.cos(angles), 0.0).astype(jnp.bfloat16)
    sin_part = jnp.where(usable, jnp.sin(angles), 0.0).astype(jnp.bfloat16)
    return jnp.concatenate([cos_part, sin_part], axis=1)


def any_rows_body(grid_values, quad_weights, owner_map, legendre, diffusion):
    channels, half_total, col_dev = grid_values.shape
    groups = lax.axis_size("lat")
    device = lax.axis_index("lat")
    half_dev = half_total // groups
    lat_total = 2 * half_total
    row_width = col_dev * groups
    owned_slots = legendre.shape[0]
    wave_count = legendre.shape[1]
    wave_ids = jnp.arange(wave_count, dtype=jnp.int32)
    slot_order = jnp.argsort(owner_map, stable=True)
    inverse_order = jnp.argsort(slot_order)
    my_waves = lax.dynamic_slice_in_dim(slot_order, device * owned_slots, owned_slots)
    contract = (((0,), (1,)), ((), ()))
    first, second = pair_rows(lat_total)
    my_first = lax.dynamic_slice_in_dim(first, device * half_dev, half_dev)
    my_second = lax.dynamic_slice_in_dim(second, device * half_dev, half_dev)
    first_len = row_length(my_first, lat_total)
    second_len = row_length(my_second, lat_total)
    first_weight = jnp.take(quad_weights, my_first)
    second_weight = jnp.take(quad_weights, my_second)

    def pair_tables(packed):
        len_a, len_b = packed
        return jnp.concatenate(
            [
                trig_table(len_a, 0, row_width, wave_ids),
                trig_table(len_b, len_a, row_width, wave_ids),
            ],
            axis=1,
        )

    all_tables = lax.map(pair_tables, (first_len, second_len))

    def forward_pair(row_data, tables):
        totals = lax.dot_general(tables, row_data, contract, preferred_element_type=jnp.float32)
        return (totals[: 2 * wave_count], totals[2 * wave_count :])

    def inverse_pair(coeffs_a, coeffs_b, tables):
        joined = jnp.concatenate([coeffs_a, coeffs_b], axis=0)
        return lax.dot_general(joined, tables, contract, preferred_element_type=jnp.float32).astype(
            jnp.bfloat16
        )

    def scaled(totals, weight, length):
        row_scale = weight / length.astype(jnp.float32)
        return jnp.concatenate(
            [totals[:wave_count] * row_scale, totals[wave_count:] * -row_scale], axis=0
        ).astype(jnp.bfloat16)

    def forward_one_pair(packed):
        row_data, tables, len_a, len_b, weight_a, weight_b = packed
        totals_a, totals_b = forward_pair(row_data, tables)
        return jnp.stack([scaled(totals_a, weight_a, len_a), scaled(totals_b, weight_b, len_b)])

    per_pair = lax.map(
        forward_one_pair,
        (
            jnp.moveaxis(
                lax.all_to_all(grid_values, "lat", split_axis=1, concat_axis=2, tiled=True), 1, 0
            ),
            all_tables,
            first_len,
            second_len,
            first_weight,
            second_weight,
        ),
    )
    per_lat = per_pair.transpose(1, 0, 2, 3).reshape(2 * half_dev, 2, wave_count, -1)
    fourier = per_lat.transpose(2, 1, 3, 0)
    picked = fourier[slot_order]
    rates = jnp.repeat(diffusion, LEVELS)
    degree = jnp.arange(wave_count, dtype=jnp.int32)
    ladder = (degree * (degree + 1)).astype(jnp.float32)
    factor = 1.0 / (1.0 + rates[:, None] * (ladder[None, :] / float(wave_count * (wave_count - 1))))
    damping = jnp.where((degree[None, :] >= my_waves[:, None])[:, None, :], factor[None, :, :], 0.0)
    spectral = jnp.einsum(
        "snl,spcl->spcn",
        legendre,
        lax.all_to_all(picked, "lat", split_axis=0, concat_axis=3, tiled=True),
        preferred_element_type=jnp.float32,
    )
    filtered = (spectral * damping[:, None, :, :]).astype(jnp.bfloat16)
    back = jnp.einsum("snl,spcn->spcl", legendre, filtered, preferred_element_type=jnp.float32)
    returned = back.astype(jnp.bfloat16)
    double = jnp.where(wave_ids == 0, 1.0, 2.0).astype(jnp.bfloat16)
    by_wave = lax.all_to_all(returned, "lat", split_axis=3, concat_axis=0, tiled=True)[
        inverse_order
    ]
    real_part = by_wave[:, 0] * double[:, None, None]
    imag_part = -(by_wave[:, 1] * double[:, None, None])
    stacked = jnp.concatenate([real_part, imag_part], axis=0)

    def backward_one_pair(packed):
        coeffs_a, coeffs_b, tables, len_a, len_b = packed
        return inverse_pair(coeffs_a, coeffs_b, tables)

    per_pair = lax.map(
        backward_one_pair,
        (
            jnp.moveaxis(stacked[:, :, :half_dev], 2, 0),
            jnp.moveaxis(stacked[:, :, half_dev:], 2, 0),
            all_tables,
            first_len,
            second_len,
        ),
    )
    rows_out = jnp.moveaxis(per_pair, 0, 1)
    return lax.all_to_all(rows_out, "lat", split_axis=2, concat_axis=1, tiled=True)


SIN_POLY = (4.44288291912434, -7.30824568650904, 3.60635421843265, -0.846111650373064, 0.1098245164248)
COS_POLY = (1.41421349625523, -6.97885094856382, 5.73946037690726, -1.88355790598724, 0.310688027527717)
LANES = 128
SUB = 8
HOPS = (0, 1, 2, 3)
SUM_ORDER = (3, 1, 2, 0)
GATHER_ORDER = (1, 3, 2)
F32 = jnp.float32
BF16 = jnp.bfloat16


def horner(poly, u):
    total = poly[-1]
    for term in poly[-2::-1]:
        total = total * u + term
    return total


def iota(shape, axis):
    return lax.broadcasted_iota(jnp.int32, shape, axis)


def swap_blocks(v):
    sub = iota(v.shape, 1)
    lane = iota(v.shape, 2)
    for bit in range(3):
        step = 1 << bit
        row_bit = (sub >> bit) & 1
        lane_bit = (lane >> (3 + bit)) & 1
        up = pltpu.roll(pltpu.roll(v, SUB - step, 1), SUB * step, 2)
        down = pltpu.roll(pltpu.roll(v, step, 1), LANES - SUB * step, 2)
        v = jnp.where(row_bit == lane_bit, v, jnp.where(row_bit == 0, up, down))
    return v


def pack_kernel(x_ref, o_ref):
    cols, channels, rows = x_ref.shape
    half = channels // 2
    x = x_ref[...].astype(F32)
    v = swap_blocks(jnp.concatenate([x[:, :half], x[:, half:]], axis=2))
    o_ref[...] = v.reshape(cols * SUB, LANES).astype(BF16)


def unpack_kernel(*refs):
    o_ref = refs[-1]
    cols, channels, rows = o_ref.shape
    total = refs[0][...].astype(F32)
    for x_ref in refs[1:-1]:
        total = total + x_ref[...].astype(F32)
    v = swap_blocks(total.reshape(cols, SUB, LANES))
    o_ref[...] = jnp.concatenate([v[:, :, :rows], v[:, :, rows:]], axis=1).astype(BF16)


def join_kernel(order, x_ref, y_ref, *o_refs):
    for i, o_ref in zip(order, o_refs):
        o_ref[...] = (x_ref[i].astype(F32) + y_ref[i].astype(F32)).astype(BF16)


def end_kernel(i, x_ref, y_ref, z_ref, o_ref):
    o_ref[...] = (x_ref[i].astype(F32) + y_ref[i].astype(F32) + z_ref[...].astype(F32)).astype(BF16)


def row_lengths(r, half_total):
    quarter = half_total // 2
    lat_total = 2 * half_total
    north = r < quarter
    first = jnp.where(north, r, half_total + r - quarter)
    second = jnp.where(north, half_total - 1 - r, lat_total - 1 - (r - quarter))
    return row_length(first, lat_total), row_length(second, lat_total)


def table_kernel(half_total, cols, waves, device_ref, owner_ref, tt_ref, wave_ref, jf_ref):
    points = tt_ref.shape[1]
    slots = wave_ref.shape[0]
    line = points // (4 * cols)
    device = device_ref[0]
    low = waves // 2
    owned = jnp.where(owner_ref[:, :low] == device, 1.0, 0.0)
    owned = jnp.broadcast_to(owned, (LANES, low)).T
    below = jnp.where(iota((low, low), 1) <= iota((low, low), 0), 1.0, 0.0).astype(BF16)
    count = jnp.dot(below, owned.astype(BF16), preferred_element_type=F32)
    wave_id = iota((low, LANES), 0).astype(F32)
    lane_slot = (iota((low, LANES), 1) % slots).astype(F32)
    hit = (owned > 0.5) & (count - 1.0 == lane_slot)
    wave = jnp.sum(jnp.where(hit, wave_id, 0.0), axis=0, keepdims=True)
    wave_ref[...] = jnp.broadcast_to(wave, (LANES, LANES)).T[:slots]
    place = iota((points, LANES), 0)
    origin = jnp.floor((place.astype(F32) + 0.5) * (1.0 / cols)).astype(jnp.int32)
    rest = place - origin * cols
    part = origin // line
    line_id = origin - part * line
    part = jnp.where(part < 2, 2 * part + 1, 2 * part - 4)
    hop = sum(jnp.where(line_id == i, HOPS[i], 0) for i in range(1, line))
    step = hop * 4 + (part & 1) * 2 + part // 2
    column = (device ^ step) * cols + rest
    jf_ref[...] = column.astype(F32)

    def block(t, carry):
        r = SUB * t + iota((1, LANES), 1) // slots
        len_a, len_b = row_lengths(r, half_total)
        len_a = len_a.astype(F32)
        len_b = len_b.astype(F32)
        rate_a = wave / len_a
        rate_b = wave / len_b
        end_a = jnp.where(2.0 * wave < len_a, len_a, 0.0)
        end_b = jnp.where(2.0 * wave < len_b, len_a + len_b, 0.0)
        for chunk in range(points // 16):
            span = slice(16 * chunk, 16 * chunk + 16)
            jf = jf_ref[span]
            in_a = jf < len_a
            turns = jnp.where(in_a, jf, jf - len_a) * jnp.where(in_a, rate_a, rate_b)
            part = turns - jnp.round(turns)
            square = part * part
            half_sin = part * horner(SIN_POLY, square)
            half_cos = horner(COS_POLY, square)
            cos_part = 1.0 - half_sin * half_sin
            sin_part = half_sin * half_cos
            use_a = jf < end_a
            use_b = (jf < end_b) & jnp.logical_not(in_a)
            tt_ref[t, span, 0:LANES] = jnp.where(use_a, cos_part, 0.0).astype(BF16)
            tt_ref[t, span, LANES : 2 * LANES] = jnp.where(use_a, sin_part, 0.0).astype(BF16)
            tt_ref[t, span, 2 * LANES : 3 * LANES] = jnp.where(use_b, cos_part, 0.0).astype(BF16)
            tt_ref[t, span, 3 * LANES : 4 * LANES] = jnp.where(use_b, sin_part, 0.0).astype(BF16)
        return carry

    lax.fori_loop(0, half_total // SUB, block, 0)


def turn_kernel(half_total, tt_ref, weight_ref, rate_ref, tr_ref, scale_ref, factor_ref):
    lat_total = 2 * half_total
    waves = factor_ref.shape[0]

    def block(t, carry):
        for i in range(4):
            lanes = slice(i * LANES, (i + 1) * LANES)
            tr_ref[t, lanes, :] = tt_ref[t, :, lanes].T
        return carry

    lax.fori_loop(0, half_total // SUB, block, 0)
    weight = jnp.broadcast_to(weight_ref[...], (LANES, lat_total)).T
    scale = weight / row_length(iota((lat_total, LANES), 0), lat_total).astype(F32)
    keep = iota((SUB, LANES), 1) % SUB == iota((SUB, LANES), 0)
    quarter = half_total // 2
    for t in range(half_total // SUB):
        r = SUB * t
        if r < quarter:
            first, second = r, half_total - 1 - r
        else:
            first, second = half_total + r - quarter, lat_total - 1 - (r - quarter)
        under = scale[second - SUB + 1 : second + 1]
        under = jnp.concatenate([under[SUB - 1 - i : SUB - i] for i in range(SUB)], axis=0)
        scale_ref[2 * t] = jnp.where(keep, scale[first : first + SUB], 0.0)
        scale_ref[2 * t + 1] = jnp.where(keep, under, 0.0)
    fields = rate_ref.shape[1]
    field = iota((1, LANES), 1) % (LANES // SUB) // LEVELS
    rate = jnp.zeros((1, LANES), F32)
    for i in range(fields):
        rate = jnp.where(field == i, rate_ref[:, i : i + 1], rate)
    degree = iota((waves, LANES), 0)
    ladder = (degree * (degree + 1)).astype(F32) / float(waves * (waves - 1))
    factor_ref[...] = 1.0 / (1.0 + rate * ladder)


def main_kernel(
    x0_ref, x1_ref, x2_ref, x3_ref, tt_ref, tr_ref, wave_ref, scale_ref, factor_ref, leg_ref, o1_ref, o3_ref, rhs_ref, z_ref, at_ref, bt_ref
):
    blocks, points, _ = tt_ref.shape
    slots, waves, lat_total = leg_ref.shape
    line, lines, _ = x0_ref.shape
    for i, x_ref in enumerate((x1_ref, x3_ref, x0_ref, x2_ref)):
        for j in range(line):
            z_ref[(i * line + j) * lines : (i * line + j + 1) * lines] = x_ref[j].astype(F32)
    row2 = iota((2 * LANES, LANES), 0)
    col2 = iota((2 * LANES, LANES), 1)
    gather = jnp.where(row2 // SUB == col2, jnp.where(row2 < LANES, 1.0, -1.0), 0.0).astype(BF16)
    wide = 2 * LANES // SUB
    row3 = iota((wide, 2 * LANES), 0)
    col3 = iota((wide, 2 * LANES), 1)
    spread = jnp.where(col3 // SUB == row3, jnp.where(col3 < LANES, 1.0, -1.0), 0.0).astype(BF16)
    slab = SUB * slots // 2

    def forward(t, carry):
        z = z_ref[pl.ds(t, points, stride=SUB), :].astype(BF16)
        d = jnp.dot(tr_ref[t], z, preferred_element_type=F32)
        for h in range(2):
            parts = []
            for p in range(2):
                base = (2 * h + p) * LANES
                rows = [
                    d[base + i * slots : base + (i + 1) * slots] * scale_ref[2 * t + h, i : i + 1, :]
                    for i in range(SUB)
                ]
                parts.append(jnp.concatenate(rows, axis=0).astype(BF16))
            a = jnp.dot(jnp.concatenate(parts, axis=1), gather, preferred_element_type=F32)
            for i in range(2):
                at_ref[pl.ds(pl.multiple_of((2 * t + i) * LANES + h * slab, SUB), slab), :] = a[i * slab : (i + 1) * slab]
        return carry

    lax.fori_loop(0, blocks, forward, 0, unroll=8)
    degree = iota((waves, LANES), 0).astype(F32)

    def slot(s, carry):
        f = at_ref[pl.ds(s, lat_total, stride=slots), :].astype(BF16)
        table = leg_ref[s]
        spectral = jnp.dot(table, f, preferred_element_type=F32)
        wave = wave_ref[pl.ds(s, 1), :]
        kept = jnp.where(degree >= wave, spectral * factor_ref[...], 0.0).astype(BF16)
        back = lax.dot_general(table, kept, (((0,), (0,)), ((), ())), preferred_element_type=F32)
        back = back.astype(BF16).astype(F32) * jnp.where(wave == 0.0, 1.0, 2.0)
        bt_ref[pl.ds(s, lat_total, stride=slots), :] = back
        return carry

    lax.fori_loop(0, slots, slot, 0, unroll=16)
    reach = -(points // 2) // 16 * -16
    keep = (iota((LANES, 2 * LANES), 1) % SUB) == iota((LANES, 2 * LANES), 0) // slots

    def inverse(t, carry):
        rhs = []
        for h in range(2):
            b = jnp.concatenate(
                [bt_ref[pl.ds(pl.multiple_of((2 * t + i) * LANES + h * slab, SUB), slab), :wide] for i in range(2)], axis=0
            ).astype(BF16)
            both = jnp.dot(b, spread, preferred_element_type=F32)
            both = jnp.where(keep, both, 0.0).astype(BF16)
            rhs.append(both[:, :LANES])
            rhs.append(both[:, LANES:])
        rhs = jnp.concatenate(rhs, axis=0)
        rhs_ref[t] = rhs
        out = jnp.dot(tt_ref[t, :reach], rhs, preferred_element_type=F32)
        z_ref[pl.ds(t, points // 2, stride=SUB), :] = out[: points // 2]
        return carry

    lax.fori_loop(0, blocks, inverse, 0, unroll=8)
    for i, o_ref in enumerate((o1_ref, o3_ref)):
        for j in range(line):
            o_ref[j] = z_ref[(i * line + j) * lines : (i * line + j + 1) * lines].astype(BF16)


def near_kernel(tt_ref, rhs_ref, o0_ref, o2_ref, z_ref):
    blocks, points, _ = tt_ref.shape
    line, lines, _ = o0_ref.shape
    from_row = points // 2 // 16 * 16

    def inverse(t, carry):
        out = jnp.dot(tt_ref[t, from_row:], rhs_ref[t], preferred_element_type=F32)
        z_ref[pl.ds(t, points // 2, stride=SUB), :] = out[points // 2 - from_row :]
        return carry

    lax.fori_loop(0, blocks, inverse, 0, unroll=8)
    for i, o_ref in enumerate((o0_ref, o2_ref)):
        for j in range(line):
            o_ref[j] = z_ref[(i * line + j) * lines : (i * line + j + 1) * lines].astype(BF16)


def kernel_call(body, out_shape, in_specs, scratch=(), flops=0, moved=0):
    return pl.pallas_call(
        body,
        out_shape=out_shape,
        in_specs=in_specs,
        scratch_shapes=list(scratch),
        compiler_params=pltpu.CompilerParams(vmem_limit_bytes=12 << 20),
        cost_estimate=pl.CostEstimate(flops=flops, bytes_accessed=moved, transcendentals=0),
    )


def transform_call(parts, tt, tr, wave, scale, factor, legendre):
    slots = wave.shape[0]
    waves, lat_total = legendre.shape[1:]
    line, lines, _ = parts[0].shape
    whole = pl.BlockSpec(memory_space=pltpu.VMEM)
    return pl.pallas_call(
        main_kernel,
        out_shape=[jax.ShapeDtypeStruct((line, lines, LANES), BF16)] * 2
        + [jax.ShapeDtypeStruct(tt.shape[:1] + (4 * LANES, LANES), BF16)],
        in_specs=[whole] * 10,
        out_specs=[whole] * 3,
        scratch_shapes=[
            pltpu.VMEM((4 * line * lines + SUB, LANES), F32),
            pltpu.VMEM(((lat_total + 1) * slots, LANES), F32),
            pltpu.VMEM(((lat_total + 1) * slots, LANES), F32),
        ],
        compiler_params=pltpu.CompilerParams(vmem_limit_bytes=16 << 20),
    )(*parts, tt, tr, wave, scale, factor, legendre)


def short_rows_body(grid_values, quad_weights, owner_map, legendre, diffusion):
    channels, half_total, cols = grid_values.shape
    groups = lax.axis_size("lat")
    line = groups // 4
    device = lax.axis_index("lat").astype(jnp.int32)
    waves = legendre.shape[1]
    lat_total = legendre.shape[2]
    slots = legendre.shape[0] // 2
    blocks = half_total // SUB
    points = cols * groups
    lines = cols * SUB
    whole = pl.BlockSpec(memory_space=pltpu.VMEM)
    shape = jax.ShapeDtypeStruct
    with jax.named_scope("pack"):
        mine = kernel_call(pack_kernel, shape((lines, LANES), BF16), [whole])(jnp.transpose(grid_values, (2, 0, 1)))

    def across(x, step):
        return lax.ppermute(x, "lat", [(i, i ^ step) for i in range(groups)])

    with jax.named_scope("gather_line"):
        arrived = {hop: across(mine, 4 * hop) for hop in GATHER_ORDER}
        arrived = [arrived[hop] for hop in HOPS[1:]]
    with jax.named_scope("tables"):
        tt, wave = kernel_call(
            functools.partial(table_kernel, half_total, cols, waves),
            (shape((blocks, points, 4 * LANES), BF16), shape((slots, LANES), F32)),
            [pl.BlockSpec(memory_space=pltpu.SMEM), whole],
            [pltpu.VMEM((points, LANES), F32)],
            flops=12 << 20,
            moved=3 << 20,
        )(device[None], owner_map[None, :])
        arrived, tt, wave = lax.optimization_barrier((arrived, tt, wave))
    with jax.named_scope("gather_line"):
        p0 = jnp.stack([mine] + arrived)
    with jax.named_scope("gather_plane"):
        p1 = across(p0, 2)
        tr, scale, factor = kernel_call(
            functools.partial(turn_kernel, half_total),
            (
                shape((blocks, 4 * LANES, points), BF16),
                shape((2 * blocks, SUB, LANES), F32),
                shape((waves, LANES), F32),
            ),
            [whole, whole, whole],
            flops=12 << 20,
            moved=6 << 20,
        )(tt, quad_weights[None, :], diffusion[None, :])
        half_legendre = legendre[:slots]
        p1, tr, scale, factor, half_legendre = lax.optimization_barrier((p1, tr, scale, factor, half_legendre))
        p2 = across(p0, 1)
        p3 = across(p1, 1)
    with jax.named_scope("transform"):
        s1, s3, rhs = transform_call((p0, p1, p2, p3), tt, tr, wave, scale, factor, half_legendre)
    block = shape((line, lines, LANES), BF16)
    with jax.named_scope("sum_cores"):
        r3 = across(s3, 1)
        s0, s2 = kernel_call(near_kernel, [block] * 2, [whole] * 2, [pltpu.VMEM((2 * line * lines + SUB, LANES), F32)])(tt, rhs)
        one = shape((lines, LANES), BF16)
        sums = kernel_call(functools.partial(join_kernel, SUM_ORDER), [one] * line, [whole] * 2)(s1, r3)
        r2 = across(s2, 1)
    with jax.named_scope("sum_plane"):
        sums = [across(piece, 2) for piece in sums]
    with jax.named_scope("sum_line"):
        ready = []
        for i, piece in zip(SUM_ORDER, sums):
            end = kernel_call(functools.partial(end_kernel, i), one, [whole] * 3)(s0, r2, piece)
            ready.append(across(end, 4 * HOPS[i]) if i else end)
    with jax.named_scope("unpack"):
        out = kernel_call(unpack_kernel, shape((cols, channels, half_total), BF16), [whole] * line)(*ready)
    return jnp.transpose(out, (1, 2, 0))


def body(grid_values, quad_weights, owner_map, legendre, diffusion):
    channels, half_total, cols = grid_values.shape
    slots, waves, lat_total = legendre.shape
    groups = lax.axis_size("lat")
    longest = 20 + 4 * (half_total - 1)
    short = (
        longest <= waves
        and groups >= 8
        and groups & (groups - 1) == 0
        and half_total % groups == 0
        and half_total // groups * 2 == SUB
        and groups == 4 * len(HOPS)
        and channels * SUB == LANES
        and channels * half_total == SUB * LANES
        and slots * SUB == 2 * LANES
        and lat_total == LANES
        and cols * groups % 16 == 0
    )
    if short:
        return short_rows_body(grid_values, quad_weights, owner_map, legendre, diffusion)
    return any_rows_body(grid_values, quad_weights, owner_map, legendre, diffusion)


def solution(mesh):
    return jax.shard_map(
        body,
        mesh=mesh,
        in_specs=(P("grp", None, "lat"), P(), P(), P("lat", None, None), P()),
        out_specs=P("grp", None, "lat"),
        check_vma=False,
    )
```

```python
import functools
import math

import jax
import jax.numpy as jnp
from jax import lax
from jax.experimental import pallas as pl
from jax.experimental.pallas import tpu as pltpu
from jax.sharding import PartitionSpec as P

LEVELS = 4


TWO_PI = 2.0 * math.pi


def pair_rows(lat_total):
    half = lat_total // 2
    quarter = lat_total // 4
    pair_ids = jnp.arange(half, dtype=jnp.int32)
    north = pair_ids < quarter
    shifted = pair_ids - quarter
    first = jnp.where(north, pair_ids, half + shifted)
    second = jnp.where(north, half - 1 - pair_ids, lat_total - 1 - shifted)
    return (first, second)


def row_length(lat_ids, lat_total):
    return 20 + 4 * jnp.minimum(lat_ids, lat_total - 1 - lat_ids)


def trig_table(length, offset, col_count, wave_ids):
    col_ids = jnp.arange(col_count, dtype=jnp.int32)
    local = col_ids - offset
    phases = local[:, None] * wave_ids[None, :] % length
    angles = phases.astype(jnp.float32) / length.astype(jnp.float32) * TWO_PI
    usable = (local[:, None] >= 0) & (local[:, None] < length) & (2 * wave_ids[None, :] < length)
    cos_part = jnp.where(usable, jnp.cos(angles), 0.0).astype(jnp.bfloat16)
    sin_part = jnp.where(usable, jnp.sin(angles), 0.0).astype(jnp.bfloat16)
    return jnp.concatenate([cos_part, sin_part], axis=1)


def any_rows_body(grid_values, quad_weights, owner_map, legendre, diffusion):
    channels, half_total, col_dev = grid_values.shape
    groups = lax.axis_size("lat")
    device = lax.axis_index("lat")
    half_dev = half_total // groups
    lat_total = 2 * half_total
    row_width = col_dev * groups
    owned_slots = legendre.shape[0]
    wave_count = legendre.shape[1]
    wave_ids = jnp.arange(wave_count, dtype=jnp.int32)
    slot_order = jnp.argsort(owner_map, stable=True)
    inverse_order = jnp.argsort(slot_order)
    my_waves = lax.dynamic_slice_in_dim(slot_order, device * owned_slots, owned_slots)
    contract = (((0,), (1,)), ((), ()))
    first, second = pair_rows(lat_total)
    my_first = lax.dynamic_slice_in_dim(first, device * half_dev, half_dev)
    my_second = lax.dynamic_slice_in_dim(second, device * half_dev, half_dev)
    first_len = row_length(my_first, lat_total)
    second_len = row_length(my_second, lat_total)
    first_weight = jnp.take(quad_weights, my_first)
    second_weight = jnp.take(quad_weights, my_second)

    def pair_tables(packed):
        len_a, len_b = packed
        return jnp.concatenate(
            [
                trig_table(len_a, 0, row_width, wave_ids),
                trig_table(len_b, len_a, row_width, wave_ids),
            ],
            axis=1,
        )

    all_tables = lax.map(pair_tables, (first_len, second_len))

    def forward_pair(row_data, tables):
        totals = lax.dot_general(tables, row_data, contract, preferred_element_type=jnp.float32)
        return (totals[: 2 * wave_count], totals[2 * wave_count :])

    def inverse_pair(coeffs_a, coeffs_b, tables):
        joined = jnp.concatenate([coeffs_a, coeffs_b], axis=0)
        return lax.dot_general(joined, tables, contract, preferred_element_type=jnp.float32).astype(
            jnp.bfloat16
        )

    def scaled(totals, weight, length):
        row_scale = weight / length.astype(jnp.float32)
        return jnp.concatenate(
            [totals[:wave_count] * row_scale, totals[wave_count:] * -row_scale], axis=0
        ).astype(jnp.bfloat16)

    def forward_one_pair(packed):
        row_data, tables, len_a, len_b, weight_a, weight_b = packed
        totals_a, totals_b = forward_pair(row_data, tables)
        return jnp.stack([scaled(totals_a, weight_a, len_a), scaled(totals_b, weight_b, len_b)])

    per_pair = lax.map(
        forward_one_pair,
        (
            jnp.moveaxis(
                lax.all_to_all(grid_values, "lat", split_axis=1, concat_axis=2, tiled=True), 1, 0
            ),
            all_tables,
            first_len,
            second_len,
            first_weight,
            second_weight,
        ),
    )
    per_lat = per_pair.transpose(1, 0, 2, 3).reshape(2 * half_dev, 2, wave_count, -1)
    fourier = per_lat.transpose(2, 1, 3, 0)
    picked = fourier[slot_order]
    rates = jnp.repeat(diffusion, LEVELS)
    degree = jnp.arange(wave_count, dtype=jnp.int32)
    ladder = (degree * (degree + 1)).astype(jnp.float32)
    factor = 1.0 / (1.0 + rates[:, None] * (ladder[None, :] / float(wave_count * (wave_count - 1))))
    damping = jnp.where((degree[None, :] >= my_waves[:, None])[:, None, :], factor[None, :, :], 0.0)
    spectral = jnp.einsum(
        "snl,spcl->spcn",
        legendre,
        lax.all_to_all(picked, "lat", split_axis=0, concat_axis=3, tiled=True),
        preferred_element_type=jnp.float32,
    )
    filtered = (spectral * damping[:, None, :, :]).astype(jnp.bfloat16)
    back = jnp.einsum("snl,spcn->spcl", legendre, filtered, preferred_element_type=jnp.float32)
    returned = back.astype(jnp.bfloat16)
    double = jnp.where(wave_ids == 0, 1.0, 2.0).astype(jnp.bfloat16)
    by_wave = lax.all_to_all(returned, "lat", split_axis=3, concat_axis=0, tiled=True)[
        inverse_order
    ]
    real_part = by_wave[:, 0] * double[:, None, None]
    imag_part = -(by_wave[:, 1] * double[:, None, None])
    stacked = jnp.concatenate([real_part, imag_part], axis=0)

    def backward_one_pair(packed):
        coeffs_a, coeffs_b, tables, len_a, len_b = packed
        return inverse_pair(coeffs_a, coeffs_b, tables)

    per_pair = lax.map(
        backward_one_pair,
        (
            jnp.moveaxis(stacked[:, :, :half_dev], 2, 0),
            jnp.moveaxis(stacked[:, :, half_dev:], 2, 0),
            all_tables,
            first_len,
            second_len,
        ),
    )
    rows_out = jnp.moveaxis(per_pair, 0, 1)
    return lax.all_to_all(rows_out, "lat", split_axis=2, concat_axis=1, tiled=True)


SIN_POLY = (4.44288291912434, -7.30824568650904, 3.60635421843265, -0.846111650373064, 0.1098245164248)
COS_POLY = (1.41421349625523, -6.97885094856382, 5.73946037690726, -1.88355790598724, 0.310688027527717)
LANES = 128
SUB = 8
HOPS = (0, 1, 2, 3)
SUM_ORDER = (3, 1, 2, 0)
GATHER_ORDER = (1, 3, 2)
F32 = jnp.float32
BF16 = jnp.bfloat16


def horner(poly, u):
    total = poly[-1]
    for term in poly[-2::-1]:
        total = total * u + term
    return total


def iota(shape, axis):
    return lax.broadcasted_iota(jnp.int32, shape, axis)


def swap_blocks(v):
    sub = iota(v.shape, 1)
    lane = iota(v.shape, 2)
    for bit in range(3):
        step = 1 << bit
        row_bit = (sub >> bit) & 1
        lane_bit = (lane >> (3 + bit)) & 1
        up = pltpu.roll(pltpu.roll(v, SUB - step, 1), SUB * step, 2)
        down = pltpu.roll(pltpu.roll(v, step, 1), LANES - SUB * step, 2)
        v = jnp.where(row_bit == lane_bit, v, jnp.where(row_bit == 0, up, down))
    return v


def pack_kernel(x_ref, o_ref):
    cols, channels, rows = x_ref.shape
    half = channels // 2
    x = x_ref[...].astype(F32)
    v = swap_blocks(jnp.concatenate([x[:, :half], x[:, half:]], axis=2))
    o_ref[...] = v.reshape(cols * SUB, LANES).astype(BF16)


def unpack_kernel(*refs):
    o_ref = refs[-1]
    cols, channels, rows = o_ref.shape
    total = refs[0][...].astype(F32)
    for x_ref in refs[1:-1]:
        total = total + x_ref[...].astype(F32)
    v = swap_blocks(total.reshape(cols, SUB, LANES))
    o_ref[...] = jnp.concatenate([v[:, :, :rows], v[:, :, rows:]], axis=1).astype(BF16)


def join_kernel(order, x_ref, y_ref, *o_refs):
    for i, o_ref in zip(order, o_refs):
        o_ref[...] = (x_ref[i].astype(F32) + y_ref[i].astype(F32)).astype(BF16)


def end_kernel(i, x_ref, y_ref, z_ref, o_ref):
    o_ref[...] = (x_ref[i].astype(F32) + y_ref[i].astype(F32) + z_ref[...].astype(F32)).astype(BF16)


def row_lengths(r, half_total):
    quarter = half_total // 2
    lat_total = 2 * half_total
    north = r < quarter
    first = jnp.where(north, r, half_total + r - quarter)
    second = jnp.where(north, half_total - 1 - r, lat_total - 1 - (r - quarter))
    return row_length(first, lat_total), row_length(second, lat_total)


def table_kernel(half_total, cols, waves, device_ref, owner_ref, tt_ref, wave_ref, jf_ref):
    points = tt_ref.shape[1]
    slots = wave_ref.shape[0]
    line = points // (4 * cols)
    device = device_ref[0]
    low = waves // 2
    owned = jnp.where(owner_ref[:, :low] == device, 1.0, 0.0)
    owned = jnp.broadcast_to(owned, (LANES, low)).T
    below = jnp.where(iota((low, low), 1) <= iota((low, low), 0), 1.0, 0.0).astype(BF16)
    count = jnp.dot(below, owned.astype(BF16), preferred_element_type=F32)
    wave_id = iota((low, LANES), 0).astype(F32)
    lane_slot = (iota((low, LANES), 1) % slots).astype(F32)
    hit = (owned > 0.5) & (count - 1.0 == lane_slot)
    wave = jnp.sum(jnp.where(hit, wave_id, 0.0), axis=0, keepdims=True)
    wave_ref[...] = jnp.broadcast_to(wave, (LANES, LANES)).T[:slots]
    place = iota((points, LANES), 0)
    origin = jnp.floor((place.astype(F32) + 0.5) * (1.0 / cols)).astype(jnp.int32)
    rest = place - origin * cols
    part = origin // line
    line_id = origin - part * line
    part = jnp.where(part < 2, 2 * part + 1, 2 * part - 4)
    hop = sum(jnp.where(line_id == i, HOPS[i], 0) for i in range(1, line))
    step = hop * 4 + (part & 1) * 2 + part // 2
    column = (device ^ step) * cols + rest
    jf_ref[...] = column.astype(F32)

    def block(t, carry):
        r = SUB * t + iota((1, LANES), 1) // slots
        len_a, len_b = row_lengths(r, half_total)
        len_a = len_a.astype(F32)
        len_b = len_b.astype(F32)
        rate_a = wave / len_a
        rate_b = wave / len_b
        end_a = jnp.where(2.0 * wave < len_a, len_a, 0.0)
        end_b = jnp.where(2.0 * wave < len_b, len_a + len_b, 0.0)
        for chunk in range(points // 16):
            span = slice(16 * chunk, 16 * chunk + 16)
            jf = jf_ref[span]
            in_a = jf < len_a
            turns = jnp.where(in_a, jf, jf - len_a) * jnp.where(in_a, rate_a, rate_b)
            part = turns - jnp.round(turns)
            square = part * part
            half_sin = part * horner(SIN_POLY, square)
            half_cos = horner(COS_POLY, square)
            cos_part = 1.0 - half_sin * half_sin
            sin_part = half_sin * half_cos
            use_a = jf < end_a
            use_b = (jf < end_b) & jnp.logical_not(in_a)
            tt_ref[t, span, 0:LANES] = jnp.where(use_a, cos_part, 0.0).astype(BF16)
            tt_ref[t, span, LANES : 2 * LANES] = jnp.where(use_a, sin_part, 0.0).astype(BF16)
            tt_ref[t, span, 2 * LANES : 3 * LANES] = jnp.where(use_b, cos_part, 0.0).astype(BF16)
            tt_ref[t, span, 3 * LANES : 4 * LANES] = jnp.where(use_b, sin_part, 0.0).astype(BF16)
        return carry

    lax.fori_loop(0, half_total // SUB, block, 0, unroll=2)


def turn_kernel(half_total, tt_ref, weight_ref, rate_ref, tr_ref, scale_ref, factor_ref):
    lat_total = 2 * half_total
    waves = factor_ref.shape[0]

    def block(t, carry):
        for i in range(4):
            lanes = slice(i * LANES, (i + 1) * LANES)
            tr_ref[t, lanes, :] = tt_ref[t, :, lanes].T
        return carry

    lax.fori_loop(0, half_total // SUB, block, 0, unroll=2)
    weight = jnp.broadcast_to(weight_ref[...], (LANES, lat_total)).T
    scale = weight / row_length(iota((lat_total, LANES), 0), lat_total).astype(F32)
    keep = iota((SUB, LANES), 1) % SUB == iota((SUB, LANES), 0)
    quarter = half_total // 2
    for t in range(half_total // SUB):
        r = SUB * t
        if r < quarter:
            first, second = r, half_total - 1 - r
        else:
            first, second = half_total + r - quarter, lat_total - 1 - (r - quarter)
        under = scale[second - SUB + 1 : second + 1]
        under = jnp.concatenate([under[SUB - 1 - i : SUB - i] for i in range(SUB)], axis=0)
        scale_ref[2 * t] = jnp.where(keep, scale[first : first + SUB], 0.0)
        scale_ref[2 * t + 1] = jnp.where(keep, under, 0.0)
    fields = rate_ref.shape[1]
    field = iota((1, LANES), 1) % (LANES // SUB) // LEVELS
    rate = jnp.zeros((1, LANES), F32)
    for i in range(fields):
        rate = jnp.where(field == i, rate_ref[:, i : i + 1], rate)
    degree = iota((waves, LANES), 0)
    ladder = (degree * (degree + 1)).astype(F32) / float(waves * (waves - 1))
    factor_ref[...] = 1.0 / (1.0 + rate * ladder)


def main_kernel(
    x0_ref, x1_ref, x2_ref, x3_ref, tt_ref, tr_ref, wave_ref, scale_ref, factor_ref, leg_ref, o1_ref, o3_ref, rhs_ref, z_ref, at_ref, bt_ref
):
    blocks, points, _ = tt_ref.shape
    slots, waves, lat_total = leg_ref.shape
    line, lines, _ = x0_ref.shape
    for i, x_ref in enumerate((x1_ref, x3_ref, x0_ref, x2_ref)):
        for j in range(line):
            z_ref[(i * line + j) * lines : (i * line + j + 1) * lines] = x_ref[j].astype(F32)
    row2 = iota((2 * LANES, LANES), 0)
    col2 = iota((2 * LANES, LANES), 1)
    gather = jnp.where(row2 // SUB == col2, jnp.where(row2 < LANES, 1.0, -1.0), 0.0).astype(BF16)
    wide = 2 * LANES // SUB
    row3 = iota((wide, 2 * LANES), 0)
    col3 = iota((wide, 2 * LANES), 1)
    spread = jnp.where(col3 // SUB == row3, jnp.where(col3 < LANES, 1.0, -1.0), 0.0).astype(BF16)
    slab = SUB * slots // 2

    def forward(t, carry):
        z = z_ref[pl.ds(t, points, stride=SUB), :].astype(BF16)
        d = jnp.dot(tr_ref[t], z, preferred_element_type=F32)
        for h in range(2):
            parts = []
            for p in range(2):
                base = (2 * h + p) * LANES
                rows = [
                    d[base + i * slots : base + (i + 1) * slots] * scale_ref[2 * t + h, i : i + 1, :]
                    for i in range(SUB)
                ]
                parts.append(jnp.concatenate(rows, axis=0).astype(BF16))
            a = jnp.dot(jnp.concatenate(parts, axis=1), gather, preferred_element_type=F32)
            for i in range(2):
                at_ref[pl.ds(pl.multiple_of((2 * t + i) * LANES + h * slab, SUB), slab), :] = a[i * slab : (i + 1) * slab]
        return carry

    lax.fori_loop(0, blocks, forward, 0, unroll=8)
    degree = iota((waves, LANES), 0).astype(F32)

    def slot(s, carry):
        f = at_ref[pl.ds(s, lat_total, stride=slots), :].astype(BF16)
        table = leg_ref[s]
        spectral = jnp.dot(table, f, preferred_element_type=F32)
        wave = wave_ref[pl.ds(s, 1), :]
        kept = jnp.where(degree >= wave, spectral * factor_ref[...], 0.0).astype(BF16)
        back = lax.dot_general(table, kept, (((0,), (0,)), ((), ())), preferred_element_type=F32)
        back = back.astype(BF16).astype(F32) * jnp.where(wave == 0.0, 1.0, 2.0)
        bt_ref[pl.ds(s, lat_total, stride=slots), :] = back
        return carry

    lax.fori_loop(0, slots, slot, 0, unroll=16)
    reach = -(points // 2) // 16 * -16
    keep = (iota((LANES, 2 * LANES), 1) % SUB) == iota((LANES, 2 * LANES), 0) // slots

    def inverse(t, carry):
        rhs = []
        for h in range(2):
            b = jnp.concatenate(
                [bt_ref[pl.ds(pl.multiple_of((2 * t + i) * LANES + h * slab, SUB), slab), :wide] for i in range(2)], axis=0
            ).astype(BF16)
            both = jnp.dot(b, spread, preferred_element_type=F32)
            both = jnp.where(keep, both, 0.0).astype(BF16)
            rhs.append(both[:, :LANES])
            rhs.append(both[:, LANES:])
        rhs = jnp.concatenate(rhs, axis=0)
        rhs_ref[t] = rhs
        out = jnp.dot(tt_ref[t, :reach], rhs, preferred_element_type=F32)
        z_ref[pl.ds(t, points // 2, stride=SUB), :] = out[: points // 2]
        return carry

    lax.fori_loop(0, blocks, inverse, 0, unroll=8)
    for i, o_ref in enumerate((o1_ref, o3_ref)):
        for j in range(line):
            o_ref[j] = z_ref[(i * line + j) * lines : (i * line + j + 1) * lines].astype(BF16)


def near_kernel(tt_ref, rhs_ref, o0_ref, o2_ref, z_ref):
    blocks, points, _ = tt_ref.shape
    line, lines, _ = o0_ref.shape
    from_row = points // 2 // 16 * 16

    def inverse(t, carry):
        out = jnp.dot(tt_ref[t, from_row:], rhs_ref[t], preferred_element_type=F32)
        z_ref[pl.ds(t, points // 2, stride=SUB), :] = out[points // 2 - from_row :]
        return carry

    lax.fori_loop(0, blocks, inverse, 0, unroll=8)
    for i, o_ref in enumerate((o0_ref, o2_ref)):
        for j in range(line):
            o_ref[j] = z_ref[(i * line + j) * lines : (i * line + j + 1) * lines].astype(BF16)


def kernel_call(body, out_shape, in_specs, scratch=(), flops=0, moved=0):
    return pl.pallas_call(
        body,
        out_shape=out_shape,
        in_specs=in_specs,
        scratch_shapes=list(scratch),
        compiler_params=pltpu.CompilerParams(vmem_limit_bytes=12 << 20),
        cost_estimate=pl.CostEstimate(flops=flops, bytes_accessed=moved, transcendentals=0),
    )


def transform_call(parts, tt, tr, wave, scale, factor, legendre):
    slots = wave.shape[0]
    waves, lat_total = legendre.shape[1:]
    line, lines, _ = parts[0].shape
    whole = pl.BlockSpec(memory_space=pltpu.VMEM)
    return pl.pallas_call(
        main_kernel,
        out_shape=[jax.ShapeDtypeStruct((line, lines, LANES), BF16)] * 2
        + [jax.ShapeDtypeStruct(tt.shape[:1] + (4 * LANES, LANES), BF16)],
        in_specs=[whole] * 10,
        out_specs=[whole] * 3,
        scratch_shapes=[
            pltpu.VMEM((4 * line * lines + SUB, LANES), F32),
            pltpu.VMEM(((lat_total + 1) * slots, LANES), F32),
            pltpu.VMEM(((lat_total + 1) * slots, LANES), F32),
        ],
        compiler_params=pltpu.CompilerParams(vmem_limit_bytes=16 << 20),
    )(*parts, tt, tr, wave, scale, factor, legendre)


def short_rows_body(grid_values, quad_weights, owner_map, legendre, diffusion):
    channels, half_total, cols = grid_values.shape
    groups = lax.axis_size("lat")
    line = groups // 4
    device = lax.axis_index("lat").astype(jnp.int32)
    waves = legendre.shape[1]
    lat_total = legendre.shape[2]
    slots = legendre.shape[0] // 2
    blocks = half_total // SUB
    points = cols * groups
    lines = cols * SUB
    whole = pl.BlockSpec(memory_space=pltpu.VMEM)
    shape = jax.ShapeDtypeStruct
    with jax.named_scope("pack"):
        mine = kernel_call(pack_kernel, shape((lines, LANES), BF16), [whole])(jnp.transpose(grid_values, (2, 0, 1)))

    def across(x, step):
        return lax.ppermute(x, "lat", [(i, i ^ step) for i in range(groups)])

    with jax.named_scope("gather_line"):
        arrived = {hop: across(mine, 4 * hop) for hop in GATHER_ORDER}
        arrived = [arrived[hop] for hop in HOPS[1:]]
    with jax.named_scope("tables"):
        tt, wave = kernel_call(
            functools.partial(table_kernel, half_total, cols, waves),
            (shape((blocks, points, 4 * LANES), BF16), shape((slots, LANES), F32)),
            [pl.BlockSpec(memory_space=pltpu.SMEM), whole],
            [pltpu.VMEM((points, LANES), F32)],
            flops=12 << 20,
            moved=3 << 20,
        )(device[None], owner_map[None, :])
        arrived, tt, wave = lax.optimization_barrier((arrived, tt, wave))
    with jax.named_scope("gather_line"):
        p0 = jnp.stack([mine] + arrived)
    with jax.named_scope("gather_plane"):
        p1 = across(p0, 2)
        tr, scale, factor = kernel_call(
            functools.partial(turn_kernel, half_total),
            (
                shape((blocks, 4 * LANES, points), BF16),
                shape((2 * blocks, SUB, LANES), F32),
                shape((waves, LANES), F32),
            ),
            [whole, whole, whole],
            flops=12 << 20,
            moved=6 << 20,
        )(tt, quad_weights[None, :], diffusion[None, :])
        half_legendre = legendre[:slots]
        p1, tr, scale, factor, half_legendre = lax.optimization_barrier((p1, tr, scale, factor, half_legendre))
        p2 = across(p0, 1)
        p3 = across(p1, 1)
    with jax.named_scope("transform"):
        s1, s3, rhs = transform_call((p0, p1, p2, p3), tt, tr, wave, scale, factor, half_legendre)
    block = shape((line, lines, LANES), BF16)
    with jax.named_scope("sum_cores"):
        r3 = across(s3, 1)
        s0, s2 = kernel_call(near_kernel, [block] * 2, [whole] * 2, [pltpu.VMEM((2 * line * lines + SUB, LANES), F32)])(tt, rhs)
        one = shape((lines, LANES), BF16)
        sums = kernel_call(functools.partial(join_kernel, SUM_ORDER), [one] * line, [whole] * 2)(s1, r3)
        r2 = across(s2, 1)
    with jax.named_scope("sum_plane"):
        sums = [across(piece, 2) for piece in sums]
    with jax.named_scope("sum_line"):
        ready = []
        for i, piece in zip(SUM_ORDER, sums):
            end = kernel_call(functools.partial(end_kernel, i), one, [whole] * 3)(s0, r2, piece)
            ready.append(across(end, 4 * HOPS[i]) if i else end)
    with jax.named_scope("unpack"):
        out = kernel_call(unpack_kernel, shape((cols, channels, half_total), BF16), [whole] * line)(*ready)
    return jnp.transpose(out, (1, 2, 0))


def body(grid_values, quad_weights, owner_map, legendre, diffusion):
    channels, half_total, cols = grid_values.shape
    slots, waves, lat_total = legendre.shape
    groups = lax.axis_size("lat")
    longest = 20 + 4 * (half_total - 1)
    short = (
        longest <= waves
        and groups >= 8
        and groups & (groups - 1) == 0
        and half_total % groups == 0
        and half_total // groups * 2 == SUB
        and groups == 4 * len(HOPS)
        and channels * SUB == LANES
        and channels * half_total == SUB * LANES
        and slots * SUB == 2 * LANES
        and lat_total == LANES
        and cols * groups % 16 == 0
    )
    if short:
        return short_rows_body(grid_values, quad_weights, owner_map, legendre, diffusion)
    return any_rows_body(grid_values, quad_weights, owner_map, legendre, diffusion)


def solution(mesh):
    return jax.shard_map(
        body,
        mesh=mesh,
        in_specs=(P("grp", None, "lat"), P(), P(), P("lat", None, None), P()),
        out_specs=P("grp", None, "lat"),
        check_vma=False,
    )
```
